128 devices in a mesh: dp: 4 (over z_hi, core), ctx: 32 (over y, x, z_lo).
Axes of the slice: x: 4, y: 4, z: 4 (z_hi: 2, z_lo: 2; z = z_hi * 2 + z_lo), core: 2. Of those that a mesh axis runs over, the one named last changes fastest.
Arguments:
- q_gate: bfloat16 [4, 4096, 4096], P('dp', None, 'ctx'), may hold values from -6 to 6
- k_gate: bfloat16 [4, 4096, 4096], P('dp', None, 'ctx'), may hold values from -6 to 6
- values: bfloat16 [4, 4096, 4096], P('dp', None, 'ctx'), may hold values from -6 to 6
- grad_out: bfloat16 [4, 4096, 4096], P('dp', None, 'ctx'), may hold values from -6 to 6
- filt: float32 [4096, 4096], P(None, 'ctx'), may hold values from -6 to 6
Outputs:
- grad_query: bfloat16 [4, 4096, 4096], P('dp', None, 'ctx')
- grad_key: bfloat16 [4, 4096, 4096], P('dp', None, 'ctx')
- grad_value: bfloat16 [4, 4096, 4096], P('dp', None, 'ctx')
- filter_grad: float32 [4096, 4096], P('ctx', 'dp')
The draws below stay inside these ranges and needn't reach their ends.
All inputs are finite; a program needn't handle non-finite values.
Results may differ from the reference program's by a relative error of at most 0.014.
Values may be sent and summed in bfloat16 or wider, within the bound.
No kernel may reach another device: no remote copies, remote signals or barrier semaphores. Data moves between devices by JAX's collectives and lax.ppermute only.
A program may use at most 128 MiB of HBM per device.

```python
import jax
import jax.numpy as jnp

C = 4096
LENGTH = 4096
NSEQ = 4


def level_of(stream_key, dims, split, least, top_value):
    factor_of, own = 1.0, jax.random.fold_in(stream_key, 6)
    for position, shards_of in split:
        draws = jnp.exp(jax.random.uniform(jax.random.fold_in(own, position), (shards_of,), jnp.float32, least / len(split), top_value / len(split)))
        factor_of = factor_of * jnp.repeat(draws, dims[position] // shards_of).reshape([-1 if axis == position else 1 for axis in range(len(dims))])
    return factor_of


def gaussian(key, extent, scale, most, split=(), kind=jnp.bfloat16):
    entries = scale * jax.random.normal(key, extent, jnp.float32)
    if split:
        entries = entries * level_of(key, extent, split, -0.22, 0.18)
    return jnp.clip(entries, -most, most).astype(kind)


def setup_inputs(seed: int = 0) -> dict:
    streams_of = jax.random.split(jax.random.key(seed), 6)
    return {
        "q_gate": gaussian(streams_of[0], (NSEQ, C, LENGTH), 1.0, 6.0, ((0, 4), (2, 32))),
        "k_gate": gaussian(streams_of[1], (NSEQ, C, LENGTH), 1.0, 6.0, ((0, 4), (2, 32))),
        "values": gaussian(streams_of[2], (NSEQ, C, LENGTH), 1.0, 6.0, ((0, 4), (2, 32))),
        "grad_out": gaussian(streams_of[3], (NSEQ, C, LENGTH), 1.0, 6.0, ((0, 4), (2, 32))),
        "filt": gaussian(streams_of[4], (C, LENGTH), 1.0, 6.0, ((1, 32),), jnp.float32),
    }


def multiply_round(first, second):
    return (first.astype(jnp.float32) * second.astype(jnp.float32)).astype(jnp.bfloat16)


def reference(q_gate, k_gate, values, grad_out, filt):
    mixed = multiply_round(k_gate, values)
    grad_mix = multiply_round(grad_out, q_gate)
    factor = LENGTH ** -0.5
    scaled = filt * factor
    width = 2 * LENGTH
    input_spec = jnp.fft.rfft(mixed.astype(jnp.float32), n=width, axis=-1)
    grad_spec = jnp.fft.rfft(grad_mix.astype(jnp.float32), n=width, axis=-1)
    filt_spec = jnp.fft.rfft(scaled, n=width, axis=-1)
    conv_out = jnp.fft.irfft(input_spec * filt_spec[None], n=width, axis=-1)[..., :LENGTH]
    back = jnp.fft.irfft(grad_spec * jnp.conj(filt_spec)[None], n=width, axis=-1)[..., :LENGTH]
    corr_spec = jnp.sum(jnp.conj(input_spec) * grad_spec, axis=0)
    filter_grad = jnp.fft.irfft(corr_spec, n=width, axis=-1)[..., :LENGTH] * factor
    conv_round = conv_out.astype(jnp.bfloat16)
    back_round = back.astype(jnp.bfloat16)
    grad_query = multiply_round(grad_out, conv_round)
    grad_key = multiply_round(back_round, values)
    grad_value = multiply_round(back_round, k_gate)
    return grad_query, grad_key, grad_value, filter_grad
```

```python
import math

import jax
import jax.numpy as jnp
import numpy as np
from jax import lax
from jax.experimental import pallas as pl
from jax.experimental.pallas import tpu as pltpu
from jax.sharding import PartitionSpec as P

LENGTH = 4096
LANES = 128
BLOCKS = LENGTH // LANES
NSEQ = 4
GROUP = 32
UNROLL = 2
BF16 = jnp.bfloat16
F32 = jnp.float32


def split_table(table):
    high = table.astype(jnp.bfloat16).astype(np.float64)
    return high, table - high


def make_tables():
    rows = np.arange(BLOCKS) + 0.5
    block = np.arange(BLOCKS)
    lane = np.arange(LANES)
    phase = 2.0 * math.pi * rows[:, None] * block[None, :] / (2 * BLOCKS)
    first = np.concatenate([np.cos(phase), -np.sin(phase)], axis=0)
    first_high, first_low = split_table(first)
    first_both = np.concatenate([first_high, first_low], axis=1)
    last = np.concatenate([np.cos(phase.T), -np.sin(phase.T)], axis=1)
    last_high, last_low = split_table(last)
    last_both = np.concatenate([last_high, last_low], axis=1)
    angle = 2.0 * math.pi * rows[:, None] * lane[None, :] / (2 * LENGTH)
    twist = np.stack([np.cos(angle), -np.sin(angle)])
    scale = 1.0 / (LENGTH * math.sqrt(LENGTH))
    untwist = np.stack([np.cos(angle), np.sin(angle)]) * scale
    turn = 2.0 * math.pi * (lane[:, None] * lane[None, :] % LANES) / LANES
    cosine, sine = np.cos(turn), np.sin(turn)
    second = np.block([[cosine, -sine], [sine, cosine]])
    inverse = np.block([[cosine, sine], [-sine, cosine]])
    return (
        first_both.astype(jnp.bfloat16),
        twist.astype(np.float32),
        second.astype(jnp.bfloat16),
        inverse.astype(jnp.bfloat16),
        untwist.astype(np.float32),
        last_both.astype(jnp.bfloat16),
    )


def dot(left, right):
    return jnp.dot(left, right, preferred_element_type=F32)


def turn_by(real, imag, turn_real, turn_imag):
    return real * turn_real - imag * turn_imag, real * turn_imag + imag * turn_real


def pair(real, imag):
    return jnp.concatenate([real, imag], axis=1).astype(BF16)


def channel(signals, first, twist, second, inverse, untwist, last):
    count = len(signals)
    flat = jnp.concatenate(signals, axis=1).astype(BF16)
    part = dot(first, jnp.concatenate([flat, flat], axis=0))
    lines = []
    for s in range(count):
        cols = slice(s * LANES, (s + 1) * LANES)
        lines.append(pair(*turn_by(part[:BLOCKS, cols], part[BLOCKS:, cols], *twist)))
    spectrum = dot(jnp.concatenate(lines, axis=0), second)

    def spec(s):
        rows = slice(s * BLOCKS, (s + 1) * BLOCKS)
        return spectrum[rows, :LANES], spectrum[rows, LANES:]

    filt_real, filt_imag = spec(2 * NSEQ)
    convs, backs = [], []
    corr_real = corr_imag = None
    for n in range(NSEQ):
        in_real, in_imag = spec(n)
        grad_real, grad_imag = spec(NSEQ + n)
        convs.append(pair(*turn_by(in_real, in_imag, filt_real, filt_imag)))
        backs.append(pair(*turn_by(grad_real, grad_imag, filt_real, -filt_imag)))
        real, imag = turn_by(grad_real, grad_imag, in_real, -in_imag)
        corr_real = real if corr_real is None else corr_real + real
        corr_imag = imag if corr_imag is None else corr_imag + imag
    products = jnp.concatenate(convs + backs + [pair(corr_real, corr_imag)], axis=0)
    line = dot(products, inverse)
    columns = []
    for s in range(count):
        rows = slice(s * BLOCKS, (s + 1) * BLOCKS)
        real, imag = turn_by(line[rows, :LANES], line[rows, LANES:], *untwist)
        columns.append(jnp.concatenate([real, imag], axis=0))
    flat = jnp.concatenate(columns, axis=1).astype(BF16)
    return dot(last, jnp.concatenate([flat, flat], axis=0))


def convolve_kernel(
    x_ref, h_ref, first_ref, twist_ref, second_ref, inverse_ref, untwist_ref, last_ref,
    y_ref, corr_ref, x_wide, h_wide, y_wide, corr_wide,
):
    per_block = 2 * GROUP
    stride = NSEQ * per_block
    rows = 512

    def widen(step, carry):
        at = pl.ds(step * rows, rows)
        x_wide[at, :] = x_ref[at, :].astype(F32)
        return carry

    lax.fori_loop(0, x_ref.shape[0] // rows, widen, 0)
    h_wide[...] = h_ref[...].astype(F32)

    def body(step, carry):
        for inner in range(UNROLL):
            c = step * UNROLL + inner
            where = [pl.ds(n * per_block + part * GROUP + c, BLOCKS, stride=stride) for part in range(2) for n in range(NSEQ)]
            lag = pl.ds(c, BLOCKS, stride=GROUP)
            signals = [x_wide[at, :] for at in where] + [h_wide[lag, :]]
            out = channel(
                signals, first_ref[...], (twist_ref[0], twist_ref[1]), second_ref[...], inverse_ref[...],
                (untwist_ref[0], untwist_ref[1]), last_ref[...],
            )
            for s, at in enumerate(where):
                y_wide[at, :] = out[:, s * LANES:(s + 1) * LANES]
            corr_wide[lag, :] = out[:, 2 * NSEQ * LANES:]
        return carry

    lax.fori_loop(0, GROUP // UNROLL, body, 0)

    def narrow(step, carry):
        at = pl.ds(step * rows, rows)
        y_ref[at, :] = y_wide[at, :].astype(BF16)
        return carry

    lax.fori_loop(0, y_ref.shape[0] // rows, narrow, 0)
    corr_ref[...] = corr_wide[...].astype(BF16)


def convolve(x, h):
    tables = [jnp.asarray(table) for table in make_tables()]
    vmem = pl.BlockSpec(memory_space=pltpu.VMEM)
    return pl.pallas_call(
        convolve_kernel,
        out_shape=(jax.ShapeDtypeStruct(x.shape, BF16), jax.ShapeDtypeStruct(h.shape, BF16)),
        in_specs=[vmem] * 8,
        out_specs=(vmem, vmem),
        scratch_shapes=[
            pltpu.VMEM(x.shape, F32),
            pltpu.VMEM(h.shape, F32),
            pltpu.VMEM(x.shape, F32),
            pltpu.VMEM(h.shape, F32),
        ],
        compiler_params=pltpu.CompilerParams(vmem_limit_bytes=48 * 2**20),
        cost_estimate=pl.CostEstimate(flops=10**10, bytes_accessed=5 * 2**20, transcendentals=0),
        name="convolve",
    )(x, h, *tables)


def product(first, second):
    return (first.astype(F32) * second.astype(F32)).astype(BF16)


def gate_kernel(k_ref, v_ref, q_ref, g_ref, x_ref):
    x_ref[:, :GROUP, :] = product(k_ref[...], v_ref[...])
    x_ref[:, GROUP:, :] = product(g_ref[...], q_ref[...])


def gate(k, v, q, g):
    count = k.shape[0]
    step = 16
    part = pl.BlockSpec((step, GROUP, LANES), lambda i: (i, 0, 0))
    return pl.pallas_call(
        gate_kernel,
        grid=(count // step,),
        out_shape=jax.ShapeDtypeStruct((count, 2 * GROUP, LANES), BF16),
        in_specs=[part] * 4,
        out_specs=pl.BlockSpec((step, 2 * GROUP, LANES), lambda i: (i, 0, 0)),
        compiler_params=pltpu.CompilerParams(vmem_limit_bytes=32 * 2**20),
        name="gate",
    )(k, v, q, g)


def ungate_kernel(y_ref, k_ref, v_ref, g_ref, gq_ref, gk_ref, gv_ref):
    conv, back = y_ref[:, :GROUP, :], y_ref[:, GROUP:, :]
    gq_ref[...] = product(g_ref[...], conv)
    gk_ref[...] = product(back, v_ref[...])
    gv_ref[...] = product(back, k_ref[...])


def ungate(y, k, v, g):
    count = k.shape[0]
    step = 16
    part = pl.BlockSpec((step, GROUP, LANES), lambda i: (i, 0, 0))
    return pl.pallas_call(
        ungate_kernel,
        grid=(count // step,),
        out_shape=(jax.ShapeDtypeStruct(k.shape, BF16),) * 3,
        in_specs=[pl.BlockSpec((step, 2 * GROUP, LANES), lambda i: (i, 0, 0))] + [part] * 3,
        out_specs=(part,) * 3,
        compiler_params=pltpu.CompilerParams(vmem_limit_bytes=32 * 2**20),
        name="ungate",
    )(y, k, v, g)


def shards(q_gate, k_gate, values, grad_out, filt):
    every = ("ctx", "dp")
    shape = q_gate.shape
    count = shape[1] // GROUP
    q, k, v, g = (a.reshape(count, GROUP, LANES) for a in (q_gate, k_gate, values, grad_out))
    own = lax.axis_index("dp")
    lags = lax.dynamic_index_in_dim(filt.reshape(BLOCKS, NSEQ, GROUP, LANES), own, 1, keepdims=False)
    h = lax.all_to_all(lags.astype(BF16), "ctx", 0, 0, tiled=True)
    x = lax.all_to_all(gate(k, v, q, g), every, 0, 0, tiled=True)
    y, corr = convolve(x.reshape(count * 2 * GROUP, LANES), h.reshape(BLOCKS * GROUP, LANES))
    corr = lax.all_to_all(corr.reshape(BLOCKS, GROUP, LANES), "dp", 0, 0, tiled=True)
    y = lax.all_to_all(y.reshape(count, 2 * GROUP, LANES), every, 0, 0, tiled=True)
    grads = ungate(y, k, v, g)
    corr = corr.reshape(NSEQ, BLOCKS // NSEQ, GROUP, LANES).transpose(0, 2, 1, 3)
    filter_grad = corr.reshape(NSEQ * GROUP, LENGTH // NSEQ).astype(F32)
    return tuple(grad.reshape(shape) for grad in grads) + (filter_grad,)


def solution(mesh):
    part = P("dp", None, "ctx")
    return jax.shard_map(
        shards,
        mesh=mesh,
        in_specs=(part, part, part, part, P(None, "ctx")),
        out_specs=(part, part, part, P("ctx", "dp")),
        check_vma=False,
    )
```

```python
import math

import jax
import jax.numpy as jnp
import numpy as np
from jax import lax
from jax.experimental import pallas as pl
from jax.experimental.pallas import tpu as pltpu
from jax.sharding import PartitionSpec as P

LENGTH = 4096
LANES = 128
BLOCKS = LENGTH // LANES
NSEQ = 4
OCTET = 8
OCTETS = 4
GROUP = OCTET * OCTETS
SIGNALS = 2 * NSEQ + 1
ROWS = BLOCKS * OCTET
BF16 = jnp.bfloat16
F32 = jnp.float32


def make_tables():
    rows = np.arange(BLOCKS) + 0.5
    block = np.arange(BLOCKS)
    lane = np.arange(LANES)
    eye = np.eye(OCTET)
    phase = 2.0 * math.pi * rows[:, None] * block[None, :] / (2 * BLOCKS)
    first = np.kron(np.concatenate([np.cos(phase), -np.sin(phase)], axis=0), eye)
    last = np.kron(np.concatenate([np.cos(phase.T), -np.sin(phase.T)], axis=1), eye)
    angle = np.repeat(2.0 * math.pi * rows[:, None] * lane[None, :] / (2 * LENGTH), OCTET, axis=0)
    scale = 1.0 / (LENGTH * math.sqrt(LENGTH))
    twist = np.stack([np.cos(angle), -np.sin(angle)])
    untwist = np.stack([np.cos(angle), np.sin(angle)]) * scale
    turn = 2.0 * math.pi * (lane[:, None] * lane[None, :] % LANES) / LANES
    cosine, sine = np.cos(turn), np.sin(turn)
    second = np.block([[cosine, -sine], [sine, cosine]])
    inverse = np.block([[cosine, sine], [-sine, cosine]])
    return (
        first.astype(jnp.bfloat16),
        twist.astype(np.float32),
        second.astype(jnp.bfloat16),
        inverse.astype(jnp.bfloat16),
        untwist.astype(np.float32),
        last.astype(jnp.bfloat16),
    )


def dot(left, right):
    return jnp.dot(left, right, preferred_element_type=F32)


def turn_by(real, imag, turn_real, turn_imag):
    return real * turn_real - imag * turn_imag, real * turn_imag + imag * turn_real


def pair(real, imag):
    return jnp.concatenate([real, imag], axis=1).astype(BF16)


def octet(signals, first, twist, second, inverse, untwist, last):
    part = dot(first, jnp.concatenate(signals, axis=1))
    lines = []
    for s in range(SIGNALS):
        cols = slice(s * LANES, (s + 1) * LANES)
        lines.append(pair(*turn_by(part[:ROWS, cols], part[ROWS:, cols], *twist)))
    spectrum = dot(jnp.concatenate(lines, axis=0), second)

    def spec(s):
        rows = slice(s * ROWS, (s + 1) * ROWS)
        return spectrum[rows, :LANES], spectrum[rows, LANES:]

    filt_real, filt_imag = spec(2 * NSEQ)
    convs, backs = [], []
    corr_real = corr_imag = None
    for n in range(NSEQ):
        in_real, in_imag = spec(n)
        grad_real, grad_imag = spec(NSEQ + n)
        convs.append(pair(*turn_by(in_real, in_imag, filt_real, filt_imag)))
        backs.append(pair(*turn_by(grad_real, grad_imag, filt_real, -filt_imag)))
        real, imag = turn_by(grad_real, grad_imag, in_real, -in_imag)
        corr_real = real if corr_real is None else corr_real + real
        corr_imag = imag if corr_imag is None else corr_imag + imag
    line = dot(jnp.concatenate(convs + backs + [pair(corr_real, corr_imag)], axis=0), inverse)
    columns = []
    for s in range(SIGNALS):
        rows = slice(s * ROWS, (s + 1) * ROWS)
        real, imag = turn_by(line[rows, :LANES], line[rows, LANES:], *untwist)
        columns.append(jnp.concatenate([real, imag], axis=0))
    return dot(last, jnp.concatenate(columns, axis=1).astype(BF16))


def convolve_kernel(
    x_ref, h_ref, first_ref, twist_ref, second_ref, inverse_ref, untwist_ref, last_ref, y_ref, corr_ref,
):
    def rows_of(piece):
        return piece.astype(F32).reshape(ROWS, LANES).astype(BF16)

    signals = [rows_of(x_ref[:, n, part]) for part in range(2) for n in range(NSEQ)]
    signals.append(rows_of(h_ref[:, 0, 0]))
    out = octet(
        signals, first_ref[...], (twist_ref[0], twist_ref[1]), second_ref[...], inverse_ref[...],
        (untwist_ref[0], untwist_ref[1]), last_ref[...],
    )

    def blocks_of(s):
        return out[:, s * LANES:(s + 1) * LANES].reshape(BLOCKS, OCTET, LANES).astype(BF16)

    for n in range(NSEQ):
        for part in range(2):
            y_ref[:, n, part] = blocks_of(part * NSEQ + n)
    corr_ref[:, 0] = blocks_of(2 * NSEQ)


def convolve(x):
    tables = [jnp.asarray(table) for table in make_tables()]
    whole = [pl.BlockSpec(table.shape, lambda j, n=table.ndim: (0,) * n) for table in tables]
    both = pl.BlockSpec((BLOCKS, NSEQ, 2, OCTET, LANES), lambda j: (0, 0, j, 0, 0))
    return pl.pallas_call(
        convolve_kernel,
        grid=(OCTETS,),
        out_shape=(
            jax.ShapeDtypeStruct((BLOCKS, NSEQ, 2 * OCTETS, OCTET, LANES), BF16),
            jax.ShapeDtypeStruct((BLOCKS, OCTETS, OCTET, LANES), BF16),
        ),
        in_specs=[both, pl.BlockSpec((BLOCKS, 1, 1, OCTET, LANES), lambda j: (0, j, 2 * OCTETS, 0, 0))] + whole,
        out_specs=(both, pl.BlockSpec((BLOCKS, 1, OCTET, LANES), lambda j: (0, j, 0, 0))),
        compiler_params=pltpu.CompilerParams(vmem_limit_bytes=58 * 2**20),
        cost_estimate=pl.CostEstimate(flops=10**10, bytes_accessed=5 * 2**20, transcendentals=0),
        name="convolve",
    )(x, x, *tables)


def product(first, second):
    return first.astype(F32) * second.astype(F32)


def gate_kernel(own_ref, k_ref, v_ref, q_ref, g_ref, filt_ref, x_ref):
    mixed = product(k_ref[...], v_ref[...])
    grad_mix = product(g_ref[...], q_ref[...])
    for j in range(OCTETS):
        rows = slice(j * OCTET, (j + 1) * OCTET)
        x_ref[:, 2 * j] = mixed[:, rows].astype(BF16)
        x_ref[:, 2 * j + 1] = grad_mix[:, rows].astype(BF16)
    x_ref[:, 2 * OCTETS] = filt_ref[:, 0].astype(BF16)


def gate(own, k, v, q, g, filt):
    count = k.shape[0]
    step = 16
    part = pl.BlockSpec((step, GROUP, LANES), lambda i, own: (i, 0, 0))
    return pl.pallas_call(
        gate_kernel,
        out_shape=jax.ShapeDtypeStruct((count, SIGNALS, OCTET, LANES), BF16),
        grid_spec=pltpu.PrefetchScalarGridSpec(
            num_scalar_prefetch=1,
            grid=(count // step,),
            in_specs=[part] * 4 + [pl.BlockSpec((step, 1, OCTET, LANES), lambda i, own: (i, own[0], 0, 0))],
            out_specs=pl.BlockSpec((step, SIGNALS, OCTET, LANES), lambda i, own: (i, 0, 0, 0)),
        ),
        compiler_params=pltpu.CompilerParams(vmem_limit_bytes=58 * 2**20),
        name="gate",
    )(own, k, v, q, g, filt)


def ungate_kernel(y_ref, k_ref, v_ref, g_ref, gq_ref, gk_ref, gv_ref):
    conv = jnp.concatenate([y_ref[:, 2 * j].astype(F32) for j in range(OCTETS)], axis=1)
    back = jnp.concatenate([y_ref[:, 2 * j + 1].astype(F32) for j in range(OCTETS)], axis=1)
    gq_ref[...] = product(g_ref[...], conv).astype(BF16)
    gk_ref[...] = product(back, v_ref[...]).astype(BF16)
    gv_ref[...] = product(back, k_ref[...]).astype(BF16)


def ungate(y, k, v, g):
    count = k.shape[0]
    step = 16
    part = pl.BlockSpec((step, GROUP, LANES), lambda i: (i, 0, 0))
    return pl.pallas_call(
        ungate_kernel,
        grid=(count // step,),
        out_shape=(jax.ShapeDtypeStruct(k.shape, BF16),) * 3,
        in_specs=[pl.BlockSpec((step, 2 * OCTETS, OCTET, LANES), lambda i: (i, 0, 0, 0))] + [part] * 3,
        out_specs=(part,) * 3,
        compiler_params=pltpu.CompilerParams(vmem_limit_bytes=58 * 2**20),
        name="ungate",
    )(y, k, v, g)


def exchange_lags(corr, own):
    quarters = corr.reshape(NSEQ, BLOCKS // NSEQ, GROUP, LANES)
    got = [lax.dynamic_index_in_dim(quarters, own, 0, keepdims=False)]
    for shift in range(1, NSEQ):
        sent = lax.dynamic_index_in_dim(quarters, own ^ shift, 0, keepdims=False)
        got.append(lax.ppermute(sent, "dp", [(d, d ^ shift) for d in range(NSEQ)]))
    odd, high = own & 1, own & 2
    got = [jnp.where(odd == 1, got[s ^ 1], got[s]) for s in range(NSEQ)]
    got = [jnp.where(high == 2, got[s ^ 2], got[s]) for s in range(NSEQ)]
    merged = jnp.stack(got).transpose(0, 2, 1, 3)
    return merged.reshape(NSEQ * GROUP, LENGTH // NSEQ).astype(F32)


def shards(q_gate, k_gate, values, grad_out, filt):
    every = ("ctx", "dp")
    shape = q_gate.shape
    count = shape[1] // GROUP
    q, k, v, g = (a.reshape(count, GROUP, LANES) for a in (q_gate, k_gate, values, grad_out))
    own = lax.axis_index("dp")
    x = gate(own.reshape(1), k, v, q, g, filt.reshape(count, OCTETS, OCTET, LANES))
    x = lax.all_to_all(x, every, 0, 0, tiled=True)
    y, corr = convolve(x.reshape(BLOCKS, NSEQ, SIGNALS, OCTET, LANES))
    y = lax.all_to_all(y.reshape(count, 2 * OCTETS, OCTET, LANES), every, 0, 0, tiled=True)
    filter_grad = exchange_lags(corr, own)
    grads = ungate(y, k, v, g)
    return tuple(grad.reshape(shape) for grad in grads) + (filter_grad,)


def solution(mesh):
    part = P("dp", None, "ctx")
    return jax.shard_map(
        shards,
        mesh=mesh,
        in_specs=(part, part, part, part, P(None, "ctx")),
        out_specs=(part, part, part, P("ctx", "dp")),
        check_vma=False,
    )
```

```python
import math

import jax
import jax.numpy as jnp
import numpy as np
from jax import lax
from jax.experimental import pallas as pl
from jax.experimental.pallas import tpu as pltpu
from jax.sharding import PartitionSpec as P

LENGTH = 4096
LANES = 128
BLOCKS = LENGTH // LANES
NSEQ = 4
OCTET = 8
OCTETS = 4
GROUP = OCTET * OCTETS
SIGNALS = 2 * NSEQ + 1
ROWS = BLOCKS * OCTET
BF16 = jnp.bfloat16
F32 = jnp.float32


def make_tables():
    rows = np.arange(BLOCKS) + 0.5
    block = np.arange(BLOCKS)
    lane = np.arange(LANES)
    eye = np.eye(OCTET)
    phase = 2.0 * math.pi * rows[:, None] * block[None, :] / (2 * BLOCKS)
    first = np.kron(np.concatenate([np.cos(phase), -np.sin(phase)], axis=0), eye)
    last = np.kron(np.concatenate([np.cos(phase.T), -np.sin(phase.T)], axis=1), eye)
    angle = np.repeat(2.0 * math.pi * rows[:, None] * lane[None, :] / (2 * LENGTH), OCTET, axis=0)
    scale = 1.0 / (LENGTH * math.sqrt(LENGTH))
    twist = np.stack([np.cos(angle), -np.sin(angle)])
    untwist = np.stack([np.cos(angle), np.sin(angle)]) * scale
    turn = 2.0 * math.pi * (lane[:, None] * lane[None, :] % LANES) / LANES
    cosine, sine = np.cos(turn), np.sin(turn)
    second = np.block([[cosine, -sine], [sine, cosine]])
    inverse = np.block([[cosine, sine], [-sine, cosine]])
    return (
        first.astype(jnp.bfloat16),
        twist.astype(np.float32),
        second.astype(jnp.bfloat16),
        inverse.astype(jnp.bfloat16),
        untwist.astype(np.float32),
        last.astype(jnp.bfloat16),
    )


def dot(left, right):
    return jnp.dot(left, right, preferred_element_type=F32)


def turn_by(real, imag, turn_real, turn_imag):
    return real * turn_real - imag * turn_imag, real * turn_imag + imag * turn_real


def pair(real, imag):
    return jnp.concatenate([real, imag], axis=1).astype(BF16)


def octet(signals, first, twist, second, inverse, untwist, last):
    part = dot(first, jnp.concatenate(signals, axis=1))
    lines = []
    for s in range(SIGNALS):
        cols = slice(s * LANES, (s + 1) * LANES)
        lines.append(pair(*turn_by(part[:ROWS, cols], part[ROWS:, cols], *twist)))
    spectrum = dot(jnp.concatenate(lines, axis=0), second)

    def spec(s):
        rows = slice(s * ROWS, (s + 1) * ROWS)
        return spectrum[rows, :LANES], spectrum[rows, LANES:]

    filt_real, filt_imag = spec(2 * NSEQ)
    convs, backs = [], []
    corr_real = corr_imag = None
    for n in range(NSEQ):
        in_real, in_imag = spec(n)
        grad_real, grad_imag = spec(NSEQ + n)
        convs.append(pair(*turn_by(in_real, in_imag, filt_real, filt_imag)))
        backs.append(pair(*turn_by(grad_real, grad_imag, filt_real, -filt_imag)))
        real, imag = turn_by(grad_real, grad_imag, in_real, -in_imag)
        corr_real = real if corr_real is None else corr_real + real
        corr_imag = imag if corr_imag is None else corr_imag + imag
    line = dot(jnp.concatenate(convs + backs + [pair(corr_real, corr_imag)], axis=0), inverse)
    columns = []
    for s in range(SIGNALS):
        rows = slice(s * ROWS, (s + 1) * ROWS)
        real, imag = turn_by(line[rows, :LANES], line[rows, LANES:], *untwist)
        columns.append(jnp.concatenate([real, imag], axis=0))
    return dot(last, jnp.concatenate(columns, axis=1).astype(BF16))


def convolve_kernel(
    x_ref, first_ref, twist_ref, second_ref, inverse_ref, untwist_ref, last_ref, y_ref, corr_ref,
):
    j = pl.program_id(0)

    def rows_of(piece):
        return piece.astype(F32).reshape(ROWS, LANES).astype(BF16)

    signals = [rows_of(x_ref[:, n, 2 * j + part]) for part in range(2) for n in range(NSEQ)]
    signals.append(rows_of(x_ref[:, j, 2 * OCTETS]))
    out = octet(
        signals, first_ref[...], (twist_ref[0], twist_ref[1]), second_ref[...], inverse_ref[...],
        (untwist_ref[0], untwist_ref[1]), last_ref[...],
    )

    def blocks_of(s):
        return out[:, s * LANES:(s + 1) * LANES].reshape(BLOCKS, OCTET, LANES).astype(BF16)

    for n in range(NSEQ):
        for part in range(2):
            y_ref[:, n, part] = blocks_of(part * NSEQ + n)
    corr_ref[:, 0] = blocks_of(2 * NSEQ)


def whole():
    return pl.BlockSpec(memory_space=pltpu.VMEM)


def convolve(x):
    tables = [jnp.asarray(table) for table in make_tables()]
    return pl.pallas_call(
        convolve_kernel,
        grid=(OCTETS,),
        out_shape=(
            jax.ShapeDtypeStruct((BLOCKS, NSEQ, 2 * OCTETS, OCTET, LANES), BF16),
            jax.ShapeDtypeStruct((BLOCKS, OCTETS, OCTET, LANES), BF16),
        ),
        in_specs=[whole()] * (1 + len(tables)),
        out_specs=(
            pl.BlockSpec((BLOCKS, NSEQ, 2, OCTET, LANES), lambda j: (0, 0, j, 0, 0)),
            pl.BlockSpec((BLOCKS, 1, OCTET, LANES), lambda j: (0, j, 0, 0)),
        ),
        compiler_params=pltpu.CompilerParams(vmem_limit_bytes=40 * 2**20),
        cost_estimate=pl.CostEstimate(flops=10**10, bytes_accessed=5 * 2**20, transcendentals=0),
        name="convolve",
    )(x, *tables)


def product(first, second):
    return first.astype(F32) * second.astype(F32)


PARTS = 4


def gate_kernel(own_ref, k_ref, v_ref, q_ref, g_ref, filt_ref, x_ref, k_in, v_in, q_in, g_in, filt_in, x_out, in_sem, filt_sem, out_sem):
    step = k_in.shape[0] // PARTS

    def arrive(i):
        at = pl.ds(i * step, step)
        refs = ((k_ref, k_in), (v_ref, v_in), (q_ref, q_in), (g_ref, g_in))
        copies = [pltpu.make_async_copy(a.at[at], b.at[at], in_sem.at[i, n]) for n, (a, b) in enumerate(refs)]
        return copies + [pltpu.make_async_copy(filt_ref.at[at, own_ref[0]], filt_in.at[at], filt_sem.at[i])]

    def leave(i):
        at = pl.ds(i * step, step)
        return pltpu.make_async_copy(x_out.at[at], x_ref.at[at], out_sem.at[i])

    for i in range(PARTS):
        for copy in arrive(i):
            copy.start()
    for i in range(PARTS):
        for copy in arrive(i):
            copy.wait()
        at = pl.ds(i * step, step)
        mixed = product(k_in[at], v_in[at])
        grad_mix = product(g_in[at], q_in[at])
        for j in range(OCTETS):
            rows = slice(j * OCTET, (j + 1) * OCTET)
            x_out[at, 2 * j] = mixed[:, rows].astype(BF16)
            x_out[at, 2 * j + 1] = grad_mix[:, rows].astype(BF16)
        x_out[at, 2 * OCTETS] = filt_in[at].astype(BF16)
        leave(i).start()
    for i in range(PARTS):
        leave(i).wait()


def gate(own, k, v, q, g, filt):
    count = k.shape[0]
    out = (count, SIGNALS, OCTET, LANES)
    anywhere = pl.BlockSpec(memory_space=pl.ANY)
    return pl.pallas_call(
        gate_kernel,
        out_shape=jax.ShapeDtypeStruct(out, BF16),
        in_specs=[pl.BlockSpec(memory_space=pltpu.SMEM)] + [anywhere] * 5,
        out_specs=anywhere,
        scratch_shapes=[pltpu.VMEM(k.shape, BF16)] * 4
        + [
            pltpu.VMEM((count, OCTET, LANES), F32),
            pltpu.VMEM(out, BF16),
            pltpu.SemaphoreType.DMA((PARTS, 4)),
            pltpu.SemaphoreType.DMA((PARTS,)),
            pltpu.SemaphoreType.DMA((PARTS,)),
        ],
        compiler_params=pltpu.CompilerParams(vmem_limit_bytes=58 * 2**20),
        name="gate",
    )(own, k, v, q, g, filt)


def ungate_kernel(own_ref, y_ref, k_ref, v_ref, g_ref, r0_ref, r1_ref, r2_ref, r3_ref, gq_ref, gk_ref, gv_ref, corr_ref):
    i = pl.program_id(0)
    step = gq_ref.shape[0]
    at = pl.ds(i * step, step)
    conv = jnp.concatenate([y_ref[at, 2 * j].astype(F32) for j in range(OCTETS)], axis=1)
    back = jnp.concatenate([y_ref[at, 2 * j + 1].astype(F32) for j in range(OCTETS)], axis=1)
    gq_ref[...] = product(g_ref[at], conv).astype(BF16)
    gk_ref[...] = product(back, v_ref[at]).astype(BF16)
    gv_ref[...] = product(back, k_ref[at]).astype(BF16)
    source = i ^ own_ref[0]
    for s, piece in enumerate((r0_ref, r1_ref, r2_ref, r3_ref)):

        @pl.when(source == s)
        def _(piece=piece):
            for p in range(piece.shape[0]):
                corr_ref[:, p * LANES:(p + 1) * LANES] = piece[p].astype(F32)


def ungate(own, y, k, v, g, pieces):
    count = k.shape[0]
    step = count // NSEQ
    part = pl.BlockSpec((step, GROUP, LANES), lambda i: (i, 0, 0))
    lags = LENGTH // NSEQ
    return pl.pallas_call(
        ungate_kernel,
        grid=(NSEQ,),
        out_shape=(jax.ShapeDtypeStruct(k.shape, BF16),) * 3 + (jax.ShapeDtypeStruct((NSEQ * GROUP, lags), F32),),
        in_specs=[pl.BlockSpec(memory_space=pltpu.SMEM)] + [whole()] * 8,
        out_specs=(part,) * 3 + (pl.BlockSpec((GROUP, lags), lambda i: (i, 0)),),
        compiler_params=pltpu.CompilerParams(vmem_limit_bytes=24 * 2**20),
        name="ungate",
    )(own, y, k, v, g, *pieces)


def exchange_lags(corr, own):
    quarters = corr.reshape(NSEQ, BLOCKS // NSEQ, GROUP, LANES)
    got = [lax.dynamic_index_in_dim(quarters, own, 0, keepdims=False)]
    for shift in range(1, NSEQ):
        sent = lax.dynamic_index_in_dim(quarters, own ^ shift, 0, keepdims=False)
        got.append(lax.ppermute(sent, "dp", [(d, d ^ shift) for d in range(NSEQ)]))
    return got


def shards(q_gate, k_gate, values, grad_out, filt):
    every = ("ctx", "dp")
    shape = q_gate.shape
    count = shape[1] // GROUP
    q, k, v, g = (a.reshape(count, GROUP, LANES) for a in (q_gate, k_gate, values, grad_out))
    own = lax.axis_index("dp")
    slot = own.reshape(1)
    x = gate(slot, k, v, q, g, filt.reshape(count, OCTETS, OCTET, LANES))
    x = lax.all_to_all(x, every, 0, 0, tiled=True)
    y, corr = convolve(x.reshape(BLOCKS, NSEQ, SIGNALS, OCTET, LANES))
    y = lax.all_to_all(y.reshape(count, 2 * OCTETS, OCTET, LANES), every, 0, 0, tiled=True)
    *grads, filter_grad = ungate(slot, y, k, v, g, exchange_lags(corr, own))
    return tuple(grad.reshape(shape) for grad in grads) + (filter_grad,)


def solution(mesh):
    part = P("dp", None, "ctx")
    return jax.shard_map(
        shards,
        mesh=mesh,
        in_specs=(part, part, part, part, P(None, "ctx")),
        out_specs=(part, part, part, P("ctx", "dp")),
        check_vma=False,
    )
```

```python
import math

import jax
import jax.numpy as jnp
import numpy as np
from jax import lax
from jax.experimental import pallas as pl
from jax.experimental.pallas import tpu as pltpu
from jax.sharding import Mesh, PartitionSpec as P

LENGTH = 4096
LANES = 128
BLOCKS = LENGTH // LANES
NSEQ = 4
OCTET = 8
OCTETS = 4
GROUP = OCTET * OCTETS
SIGNALS = 2 * NSEQ + 1
ROWS = BLOCKS * OCTET
BF16 = jnp.bfloat16
F32 = jnp.float32

SPLIT = {"zh": 2, "k": 2, "y": 4, "x": 4, "zl": 2}
DP, CTX = ("zh", "k"), ("y", "x", "zl")
ORDER = ("zl", "zh", "x", "k", "y")
LEAD = tuple(SPLIT[axis] for axis in ORDER)


def make_tables():
    rows = np.arange(BLOCKS) + 0.5
    block = np.array([y * 8 + x * 2 + zl for zl in range(2) for x in range(4) for y in range(4)])
    lane = np.arange(LANES)
    eye = np.eye(OCTET)
    phase = 2.0 * math.pi * rows[:, None] * block[None, :] / (2 * BLOCKS)
    first = np.stack([np.cos(phase), -np.sin(phase)], axis=1).reshape(2 * BLOCKS, BLOCKS)
    angle = np.repeat(2.0 * math.pi * rows[:, None] * lane[None, :] / (2 * LENGTH), OCTET, axis=0)
    scale = 1.0 / (LENGTH * math.sqrt(LENGTH))
    twist = np.stack([np.cos(angle), -np.sin(angle)])
    untwist = np.stack([np.cos(angle), np.sin(angle)]) * scale
    turn = 2.0 * math.pi * (lane[:, None] * lane[None, :] % LANES) / LANES
    cosine, sine = np.cos(turn), np.sin(turn)
    second = np.block([[cosine, -sine], [sine, cosine]])
    inverse = np.block([[cosine, sine], [-sine, cosine]])
    return (
        np.kron(first, eye).astype(jnp.bfloat16),
        twist.astype(np.float32),
        second.astype(jnp.bfloat16),
        inverse.astype(jnp.bfloat16),
        untwist.astype(np.float32),
        np.kron(first.T, eye).astype(jnp.bfloat16),
    )


def dot(left, right):
    return jnp.dot(left, right, preferred_element_type=F32)


def turn_by(real, imag, turn_real, turn_imag):
    return real * turn_real - imag * turn_imag, real * turn_imag + imag * turn_real


def pair(real, imag):
    return jnp.concatenate([real, imag], axis=1).astype(BF16)


def octet(signals, first, twist, second, inverse, untwist, last):
    spectra = []
    for s in range(0, SIGNALS, 2):
        both = signals[s:s + 2]
        width = len(both) * LANES
        part = dot(first, jnp.concatenate(both, axis=1)).reshape(BLOCKS, 2, OCTET, width)
        real, imag = part[:, 0].reshape(ROWS, width), part[:, 1].reshape(ROWS, width)
        for at in range(0, width, LANES):
            line = pair(*turn_by(real[:, at:at + LANES], imag[:, at:at + LANES], *twist))
            spectrum = dot(line, second)
            spectra.append((spectrum[:, :LANES], spectrum[:, LANES:]))
    filt_real, filt_imag = spectra[2 * NSEQ]
    convs, backs = [], []
    corr_real = corr_imag = None
    for n in range(NSEQ):
        in_real, in_imag = spectra[n]
        grad_real, grad_imag = spectra[NSEQ + n]
        convs.append(pair(*turn_by(in_real, in_imag, filt_real, filt_imag)))
        backs.append(pair(grad_real * filt_real + grad_imag * filt_imag, grad_imag * filt_real - grad_real * filt_imag))
        real = grad_real * in_real + grad_imag * in_imag
        imag = grad_imag * in_real - grad_real * in_imag
        corr_real = real if corr_real is None else corr_real + real
        corr_imag = imag if corr_imag is None else corr_imag + imag
    columns = []
    for product_spectrum in convs + backs + [pair(corr_real, corr_imag)]:
        line = dot(product_spectrum, inverse)
        real, imag = turn_by(line[:, :LANES], line[:, LANES:], *untwist)
        mixed = jnp.stack([real.reshape(BLOCKS, OCTET, LANES), imag.reshape(BLOCKS, OCTET, LANES)], axis=1)
        columns.append(mixed.reshape(2 * ROWS, LANES).astype(BF16))
    results = []
    for s in range(0, SIGNALS, 2):
        out = dot(last, jnp.concatenate(columns[s:s + 2], axis=1))
        results += [out[:, at:at + LANES] for at in range(0, out.shape[1], LANES)]
    return results


def convolve_kernel(
    x_ref, first_ref, twist_ref, second_ref, inverse_ref, untwist_ref, last_ref, y_ref, corr_ref,
):
    step = pl.program_id(0)

    def rows_of(piece):
        return piece.astype(F32).reshape(ROWS, LANES).astype(BF16)

    for o in range(SPLIT["k"]):
        j = step * SPLIT["k"] + o
        signals = [rows_of(x_ref[:, n // 2, :, n % 2, :, 2 * j + part]) for part in range(2) for n in range(NSEQ)]
        signals.append(rows_of(x_ref[:, step, :, o, :, 2 * OCTETS]))
        out = octet(
            signals, first_ref[...], (twist_ref[0], twist_ref[1]), second_ref[...], inverse_ref[...],
            (untwist_ref[0], untwist_ref[1]), last_ref[...],
        )
        out = [piece.reshape(2, 4, 4, OCTET, LANES).astype(BF16) for piece in out]
        for n in range(NSEQ):
            for part in range(2):
                y_ref[:, n // 2, :, n % 2, :, 2 * o + part] = out[part * NSEQ + n]
        for zl in range(2):
            for x in range(4):
                corr_ref[:, x, zl, o] = out[2 * NSEQ][zl, x]


def whole():
    return pl.BlockSpec(memory_space=pltpu.VMEM)


def convolve(x):
    tables = [jnp.asarray(table) for table in make_tables()]
    per = SPLIT["k"]
    return pl.pallas_call(
        convolve_kernel,
        grid=(OCTETS // per,),
        out_shape=(
            pltpu.HBM(LEAD + (2 * OCTETS, OCTET, LANES), BF16),
            jax.ShapeDtypeStruct((4, 4, 2, OCTETS, OCTET, LANES), BF16),
        ),
        in_specs=[whole()] * (1 + len(tables)),
        out_specs=(
            pl.BlockSpec(LEAD + (2 * per, OCTET, LANES), lambda j: (0, 0, 0, 0, 0, j, 0, 0)),
            pl.BlockSpec((4, 4, 2, per, OCTET, LANES), lambda j: (0, 0, 0, j, 0, 0)),
        ),
        compiler_params=pltpu.CompilerParams(vmem_limit_bytes=44 * 2**20),
        cost_estimate=pl.CostEstimate(flops=10**10, bytes_accessed=5 * 2**20, transcendentals=0),
        name="convolve",
    )(x, *tables)


def product(first, second):
    return first.astype(F32) * second.astype(F32)


def gate_kernel(
    own_ref, k_ref, v_ref, q_ref, g_ref, filt_ref, x_out, k_in, v_in, g_in, q_in, filt_in, in_sem, filt_sem,
):
    parts = SPLIT["y"]
    step = k_in.shape[0] // parts

    def arrive(y):
        at = pl.ds(y * step, step)
        refs = ((k_ref, k_in), (v_ref, v_in), (q_ref, q_in), (g_ref, g_in))
        copies = [pltpu.make_async_copy(a.at[at], b.at[at], in_sem.at[y, n]) for n, (a, b) in enumerate(refs)]
        return copies + [pltpu.make_async_copy(filt_ref.at[at, own_ref[0]], filt_in.at[at], filt_sem.at[y])]

    for y in range(parts):
        for copy in arrive(y):
            copy.start()
    for y in range(parts):
        for copy in arrive(y):
            copy.wait()
        at = pl.ds(y * step, step)
        mixed = product(k_in[at], v_in[at]).reshape(4, 2, 2, 2, GROUP, LANES)
        grad_mix = product(g_in[at], q_in[at]).reshape(4, 2, 2, 2, GROUP, LANES)
        lags = filt_in[at].reshape(4, 2, 2, 2, OCTET, LANES)
        for zl in range(2):
            for zh in range(2):
                for j in range(OCTETS):
                    rows = slice(j * OCTET, (j + 1) * OCTET)
                    x_out[zl, zh, :, :, y, 2 * j] = mixed[:, zl, zh, :, rows].astype(BF16)
                    x_out[zl, zh, :, :, y, 2 * j + 1] = grad_mix[:, zl, zh, :, rows].astype(BF16)
                x_out[zl, zh, :, :, y, 2 * OCTETS] = lags[:, zl, zh].astype(BF16)


def gate(own, k, v, q, g, filt):
    count = k.shape[0]
    parts = SPLIT["y"]
    far = pl.BlockSpec(memory_space=pltpu.HBM)
    kept = jax.ShapeDtypeStruct(k.shape, BF16)
    return pl.pallas_call(
        gate_kernel,
        out_shape=(jax.ShapeDtypeStruct(LEAD + (SIGNALS, OCTET, LANES), BF16), kept, kept, kept),
        in_specs=[pl.BlockSpec(memory_space=pltpu.SMEM)] + [far] * 5,
        out_specs=(whole(),) * 4,
        scratch_shapes=[
            pltpu.VMEM(k.shape, BF16),
            pltpu.VMEM((count, OCTET, LANES), F32),
            pltpu.SemaphoreType.DMA((parts, 4)),
            pltpu.SemaphoreType.DMA((parts,)),
        ],
        compiler_params=pltpu.CompilerParams(vmem_limit_bytes=24 * 2**20),
        name="gate",
    )(own, k, v, q, g, filt)


def ungate_kernel(own_ref, y_ref, k_ref, v_ref, g_ref, r0_ref, r1_ref, r2_ref, r3_ref, gq_ref, gk_ref, gv_ref, corr_ref):
    i = pl.program_id(0)
    step = gq_ref.shape[0]
    for x in range(4):
        for zl in range(2):
            for zh in range(2):
                row = x * 8 + zl * 4 + zh * 2
                here, there = pl.ds(row, 2), pl.ds(i * step + row, 2)
                conv, back = (
                    jnp.concatenate([y_ref[zl, zh, x, :, i, 2 * j + part].astype(F32) for j in range(OCTETS)], axis=1)
                    for part in range(2)
                )
                gq_ref[here] = product(g_ref[there], conv).astype(BF16)
                gk_ref[here] = product(back, v_ref[there]).astype(BF16)
                gv_ref[here] = product(back, k_ref[there]).astype(BF16)
    source = i ^ own_ref[0]
    for s, piece in enumerate((r0_ref, r1_ref, r2_ref, r3_ref)):

        @pl.when(source == s)
        def _(piece=piece):
            for p in range(piece.shape[0]):
                corr_ref[:, p * LANES:(p + 1) * LANES] = piece[p].astype(F32)


def ungate(own, y, k, v, g, pieces):
    count = k.shape[0]
    step = count // NSEQ
    part = pl.BlockSpec((step, GROUP, LANES), lambda i: (i, 0, 0))
    lags = LENGTH // NSEQ
    return pl.pallas_call(
        ungate_kernel,
        grid=(NSEQ,),
        out_shape=(jax.ShapeDtypeStruct(k.shape, BF16),) * 3 + (jax.ShapeDtypeStruct((NSEQ * GROUP, lags), F32),),
        in_specs=[pl.BlockSpec(memory_space=pltpu.SMEM)] + [whole()] * 8,
        out_specs=(part,) * 3 + (pl.BlockSpec((GROUP, lags), lambda i: (i, 0)),),
        compiler_params=pltpu.CompilerParams(vmem_limit_bytes=24 * 2**20),
        name="ungate",
    )(own, y, k, v, g, *pieces)


def exchange_lags(corr, own):
    quarters = corr.reshape(NSEQ, BLOCKS // NSEQ, GROUP, LANES)
    got = [lax.dynamic_index_in_dim(quarters, own, 0, keepdims=False)]
    for shift in range(1, NSEQ):
        sent = lax.dynamic_index_in_dim(quarters, own ^ shift, 0, keepdims=False)
        got.append(lax.ppermute(sent, DP, [(d, d ^ shift) for d in range(NSEQ)]))
    return got


def exchange(array):
    flat = array.reshape((-1,) + array.shape[len(LEAD):])
    return lax.all_to_all(flat, ORDER, 0, 0, tiled=True).reshape(array.shape)


def shards(q_gate, k_gate, values, grad_out, filt):
    shape = q_gate.shape
    count = shape[1] // GROUP
    q, k, v, g = (a.reshape(count, GROUP, LANES) for a in (q_gate, k_gate, values, grad_out))
    own = lax.axis_index(DP)
    slot = own.reshape(1)
    x, k, v, g = gate(slot, k, v, q, g, filt.reshape(count, OCTETS, OCTET, LANES))
    y, corr = convolve(exchange(x))
    *grads, filter_grad = ungate(slot, exchange(y), k, v, g, exchange_lags(corr, own))
    return tuple(grad.reshape(shape) for grad in grads) + (filter_grad,)


def solution(mesh):
    split = Mesh(mesh.devices.reshape(tuple(SPLIT.values())), tuple(SPLIT))
    part = P(DP, None, CTX)
    return jax.shard_map(
        shards,
        mesh=split,
        in_specs=(part, part, part, part, P(None, CTX)),
        out_specs=(part, part, part, P(CTX, DP)),
        check_vma=False,
    )
```

```python
import math

import jax
import jax.numpy as jnp
import numpy as np
from jax import lax
from jax.experimental import pallas as pl
from jax.experimental.pallas import tpu as pltpu
from jax.sharding import Mesh, PartitionSpec as P

LENGTH = 4096
LANES = 128
BLOCKS = LENGTH // LANES
NSEQ = 4
OCTET = 8
OCTETS = 4
GROUP = OCTET * OCTETS
SIGNALS = 2 * NSEQ + 1
ROWS = BLOCKS * OCTET
BF16 = jnp.bfloat16
F32 = jnp.float32

SPLIT = {"zh": 2, "k": 2, "y": 4, "x": 4, "zl": 2}
DP, CTX = ("zh", "k"), ("y", "x", "zl")
ORDER = ("zl", "zh", "x", "k", "y")
LEAD = tuple(SPLIT[axis] for axis in ORDER)


def make_tables():
    rows = np.arange(BLOCKS) + 0.5
    block = np.array([y * 8 + x * 2 + zl for zl in range(2) for x in range(4) for y in range(4)])
    lane = np.arange(LANES)
    eye = np.eye(OCTET)
    phase = 2.0 * math.pi * rows[:, None] * block[None, :] / (2 * BLOCKS)
    first = np.stack([np.cos(phase), -np.sin(phase)], axis=1).reshape(2 * BLOCKS, BLOCKS)
    angle = np.repeat(2.0 * math.pi * rows[:, None] * lane[None, :] / (2 * LENGTH), OCTET, axis=0)
    scale = 1.0 / (LENGTH * math.sqrt(LENGTH))
    twist = np.stack([np.cos(angle), -np.sin(angle)])
    untwist = np.stack([np.cos(angle), np.sin(angle)]) * scale
    turn = 2.0 * math.pi * (lane[:, None] * lane[None, :] % LANES) / LANES
    cosine, sine = np.cos(turn), np.sin(turn)
    second = np.block([[cosine, -sine], [sine, cosine]])
    inverse = np.block([[cosine, sine], [-sine, cosine]])
    return (
        np.kron(first, eye).astype(jnp.bfloat16),
        twist.astype(np.float32),
        second.astype(jnp.bfloat16),
        inverse.astype(jnp.bfloat16),
        untwist.astype(np.float32),
        np.kron(first.T, eye).astype(jnp.bfloat16),
    )


def dot(left, right):
    return jnp.dot(left, right, preferred_element_type=F32)


def turn_by(real, imag, turn_real, turn_imag):
    return real * turn_real - imag * turn_imag, real * turn_imag + imag * turn_real


def pair(real, imag):
    return jnp.concatenate([real, imag], axis=1).astype(BF16)


def octet(signals, first, twist, second, inverse, untwist, last):
    spectra = []
    for s in range(0, SIGNALS, 2):
        both = signals[s:s + 2]
        width = len(both) * LANES
        part = dot(first, jnp.concatenate(both, axis=1)).reshape(BLOCKS, 2, OCTET, width)
        real, imag = part[:, 0].reshape(ROWS, width), part[:, 1].reshape(ROWS, width)
        for at in range(0, width, LANES):
            line = pair(*turn_by(real[:, at:at + LANES], imag[:, at:at + LANES], *twist))
            spectrum = dot(line, second)
            spectra.append((spectrum[:, :LANES], spectrum[:, LANES:]))
    filt_real, filt_imag = spectra[2 * NSEQ]
    convs, backs = [], []
    corr_real = corr_imag = None
    for n in range(NSEQ):
        in_real, in_imag = spectra[n]
        grad_real, grad_imag = spectra[NSEQ + n]
        convs.append(pair(*turn_by(in_real, in_imag, filt_real, filt_imag)))
        backs.append(pair(grad_real * filt_real + grad_imag * filt_imag, grad_imag * filt_real - grad_real * filt_imag))
        real = grad_real * in_real + grad_imag * in_imag
        imag = grad_imag * in_real - grad_real * in_imag
        corr_real = real if corr_real is None else corr_real + real
        corr_imag = imag if corr_imag is None else corr_imag + imag
    columns = []
    for product_spectrum in convs + backs + [pair(corr_real, corr_imag)]:
        line = dot(product_spectrum, inverse)
        real, imag = turn_by(line[:, :LANES], line[:, LANES:], *untwist)
        mixed = jnp.stack([real.reshape(BLOCKS, OCTET, LANES), imag.reshape(BLOCKS, OCTET, LANES)], axis=1)
        columns.append(mixed.reshape(2 * ROWS, LANES).astype(BF16))
    results = []
    for s in range(0, SIGNALS, 2):
        out = dot(last, jnp.concatenate(columns[s:s + 2], axis=1))
        results += [out[:, at:at + LANES] for at in range(0, out.shape[1], LANES)]
    return results


def convolve_kernel(
    x_ref, first_ref, twist_ref, second_ref, inverse_ref, untwist_ref, last_ref, y_ref, corr_ref,
):
    step = pl.program_id(0)

    def rows_of(piece):
        return piece.astype(F32).reshape(ROWS, LANES).astype(BF16)

    for o in range(SPLIT["k"]):
        j = step * SPLIT["k"] + o
        signals = [rows_of(x_ref[:, n // 2, :, n % 2, :, 2 * j + part]) for part in range(2) for n in range(NSEQ)]
        signals.append(rows_of(x_ref[:, step, :, o, :, 2 * OCTETS]))
        out = octet(
            signals, first_ref[...], (twist_ref[0], twist_ref[1]), second_ref[...], inverse_ref[...],
            (untwist_ref[0], untwist_ref[1]), last_ref[...],
        )
        out = [piece.reshape(2, 4, 4, OCTET, LANES).astype(BF16) for piece in out]
        for n in range(NSEQ):
            for part in range(2):
                y_ref[:, n // 2, :, n % 2, :, 2 * o + part] = out[part * NSEQ + n]
        for zl in range(2):
            for x in range(4):
                corr_ref[:, x, zl, o] = out[2 * NSEQ][zl, x]


def whole():
    return pl.BlockSpec(memory_space=pltpu.VMEM)


def convolve(x):
    tables = [jnp.asarray(table) for table in make_tables()]
    per = SPLIT["k"]
    return pl.pallas_call(
        convolve_kernel,
        grid=(OCTETS // per,),
        out_shape=(
            pltpu.HBM(LEAD + (2 * OCTETS, OCTET, LANES), BF16),
            jax.ShapeDtypeStruct((4, 4, 2, OCTETS, OCTET, LANES), BF16),
        ),
        in_specs=[whole()] * (1 + len(tables)),
        out_specs=(
            pl.BlockSpec(LEAD + (2 * per, OCTET, LANES), lambda j: (0, 0, 0, 0, 0, j, 0, 0)),
            pl.BlockSpec((4, 4, 2, per, OCTET, LANES), lambda j: (0, 0, 0, j, 0, 0)),
        ),
        compiler_params=pltpu.CompilerParams(vmem_limit_bytes=44 * 2**20),
        cost_estimate=pl.CostEstimate(flops=10**10, bytes_accessed=5 * 2**20, transcendentals=0),
        name="convolve",
    )(x, *tables)


def product(first, second):
    return first.astype(F32) * second.astype(F32)


def gate_kernel(
    own_ref, k_ref, v_ref, q_ref, g_ref, filt_ref, x_out, k_in, v_in, q_in, g_in, filt_in, in_sem, filt_sem,
):
    parts = SPLIT["y"]
    step = k_in.shape[0] // parts

    def arrive(y):
        at = pl.ds(y * step, step)
        refs = ((k_ref, k_in), (v_ref, v_in), (q_ref, q_in), (g_ref, g_in))
        copies = [pltpu.make_async_copy(a.at[at], b.at[at], in_sem.at[y, n]) for n, (a, b) in enumerate(refs)]
        return copies + [pltpu.make_async_copy(filt_ref.at[at, own_ref[0]], filt_in.at[at], filt_sem.at[y])]

    for y in range(parts):
        for copy in arrive(y):
            copy.start()
    for y in range(parts):
        for copy in arrive(y):
            copy.wait()
        at = pl.ds(y * step, step)
        mixed = product(k_in[at], v_in[at]).reshape(4, 2, 2, 2, GROUP, LANES)
        grad_mix = product(g_in[at], q_in[at]).reshape(4, 2, 2, 2, GROUP, LANES)
        lags = filt_in[at].reshape(4, 2, 2, 2, OCTET, LANES)
        for zl in range(2):
            for zh in range(2):
                for j in range(OCTETS):
                    rows = slice(j * OCTET, (j + 1) * OCTET)
                    x_out[zl, zh, :, :, y, 2 * j] = mixed[:, zl, zh, :, rows].astype(BF16)
                    x_out[zl, zh, :, :, y, 2 * j + 1] = grad_mix[:, zl, zh, :, rows].astype(BF16)
                x_out[zl, zh, :, :, y, 2 * OCTETS] = lags[:, zl, zh].astype(BF16)


def in_hbm(array):
    return pltpu.with_memory_space_constraint(array, pltpu.HBM)


def gate(own, k, v, q, g, filt):
    count = k.shape[0]
    parts = SPLIT["y"]
    far = pl.BlockSpec(memory_space=pltpu.HBM)
    return pl.pallas_call(
        gate_kernel,
        out_shape=jax.ShapeDtypeStruct(LEAD + (SIGNALS, OCTET, LANES), BF16),
        in_specs=[pl.BlockSpec(memory_space=pltpu.SMEM)] + [far] * 5,
        out_specs=whole(),
        scratch_shapes=[pltpu.VMEM(k.shape, BF16)] * 4
        + [
            pltpu.VMEM((count, OCTET, LANES), F32),
            pltpu.SemaphoreType.DMA((parts, 4)),
            pltpu.SemaphoreType.DMA((parts,)),
        ],
        compiler_params=pltpu.CompilerParams(vmem_limit_bytes=24 * 2**20),
        name="gate",
    )(own, *(in_hbm(array) for array in (k, v, q, g, filt)))


def ungate_kernel(
    own_ref, y_ref, k_ref, v_ref, g_ref, r0_ref, r1_ref, r2_ref, r3_ref, gq_ref, gk_ref, gv_ref, corr_ref,
    k_in, v_in, g_in, r_in, gq_out, gk_out, gv_out, corr_out, in_sem, r_sem, out_sem, corr_sem,
):
    parts = SPLIT["y"]
    step = k_in.shape[0] // parts

    def arrive(i):
        at = pl.ds(i * step, step)
        refs = ((k_ref, k_in), (v_ref, v_in), (g_ref, g_in))
        return [pltpu.make_async_copy(a.at[at], b.at[at], in_sem.at[i, n]) for n, (a, b) in enumerate(refs)]

    def leave(i):
        at = pl.ds(i * step, step)
        refs = ((gq_out, gq_ref), (gk_out, gk_ref), (gv_out, gv_ref))
        return [pltpu.make_async_copy(a.at[at], b.at[at], out_sem.at[i, n]) for n, (a, b) in enumerate(refs)]

    pieces = [pltpu.make_async_copy(r, r_in.at[s], r_sem.at[s]) for s, r in enumerate((r0_ref, r1_ref, r2_ref, r3_ref))]
    for copy in pieces:
        copy.start()
    for i in range(parts):
        for copy in arrive(i):
            copy.start()
    for s, copy in enumerate(pieces):
        copy.wait()
        rows = pl.ds(pl.multiple_of((own_ref[0] ^ s) * GROUP, GROUP), GROUP)
        for p in range(BLOCKS // NSEQ):
            corr_out[rows, p * LANES:(p + 1) * LANES] = r_in[s, p].astype(F32)
    corr_copy = pltpu.make_async_copy(corr_out, corr_ref, corr_sem)
    corr_copy.start()
    for i in range(parts):
        for copy in arrive(i):
            copy.wait()
        for x in range(4):
            for zl in range(2):
                for zh in range(2):
                    at = pl.ds(i * step + x * 8 + zl * 4 + zh * 2, 2)
                    conv, back = (
                        jnp.concatenate([y_ref[zl, zh, x, :, i, 2 * j + part].astype(F32) for j in range(OCTETS)], axis=1)
                        for part in range(2)
                    )
                    gq_out[at] = product(g_in[at], conv).astype(BF16)
                    gk_out[at] = product(back, v_in[at]).astype(BF16)
                    gv_out[at] = product(back, k_in[at]).astype(BF16)
        for copy in leave(i):
            copy.start()
    for i in range(parts):
        for copy in leave(i):
            copy.wait()
    corr_copy.wait()


def ungate(own, y, k, v, g, pieces):
    parts = SPLIT["y"]
    lags = LENGTH // NSEQ
    far = pl.BlockSpec(memory_space=pltpu.HBM)
    corr_shape = (NSEQ * GROUP, lags)
    return pl.pallas_call(
        ungate_kernel,
        out_shape=(pltpu.HBM(k.shape, BF16),) * 3 + (pltpu.HBM(corr_shape, F32),),
        in_specs=[pl.BlockSpec(memory_space=pltpu.SMEM), whole()] + [far] * 7,
        out_specs=(far,) * 4,
        scratch_shapes=[pltpu.VMEM(k.shape, BF16)] * 3
        + [pltpu.VMEM((NSEQ,) + pieces[0].shape, BF16)]
        + [pltpu.VMEM(k.shape, BF16)] * 3
        + [
            pltpu.VMEM(corr_shape, F32),
            pltpu.SemaphoreType.DMA((parts, 3)),
            pltpu.SemaphoreType.DMA((NSEQ,)),
            pltpu.SemaphoreType.DMA((parts, 3)),
            pltpu.SemaphoreType.DMA,
        ],
        compiler_params=pltpu.CompilerParams(vmem_limit_bytes=24 * 2**20),
        name="ungate",
    )(own, y, *(in_hbm(array) for array in (k, v, g, *pieces)))


def exchange_lags(corr, own):
    quarters = corr.reshape(NSEQ, BLOCKS // NSEQ, GROUP, LANES)
    got = [lax.dynamic_index_in_dim(quarters, own, 0, keepdims=False)]
    for shift in range(1, NSEQ):
        sent = lax.dynamic_index_in_dim(quarters, own ^ shift, 0, keepdims=False)
        got.append(lax.ppermute(sent, DP, [(d, d ^ shift) for d in range(NSEQ)]))
    return got


def exchange(array):
    flat = array.reshape((-1,) + array.shape[len(LEAD):])
    return lax.all_to_all(flat, ORDER, 0, 0, tiled=True).reshape(array.shape)


def shards(q_gate, k_gate, values, grad_out, filt):
    shape = q_gate.shape
    count = shape[1] // GROUP
    q, k, v, g = (a.reshape(count, GROUP, LANES) for a in (q_gate, k_gate, values, grad_out))
    own = lax.axis_index(DP)
    slot = own.reshape(1)
    x = gate(slot, k, v, q, g, filt.reshape(count, OCTETS, OCTET, LANES))
    y, corr = convolve(exchange(x))
    pieces = exchange_lags(corr, own)
    *grads, filter_grad = ungate(slot, exchange(y), k, v, g, pieces)
    return tuple(grad.reshape(shape) for grad in grads) + (filter_grad,)


def solution(mesh):
    split = Mesh(mesh.devices.reshape(tuple(SPLIT.values())), tuple(SPLIT))
    part = P(DP, None, CTX)
    return jax.shard_map(
        shards,
        mesh=split,
        in_specs=(part, part, part, part, P(None, CTX)),
        out_specs=(part, part, part, P(CTX, DP)),
        check_vma=False,
    )
```

```python
import math

import jax
import jax.numpy as jnp
import numpy as np
from jax import lax
from jax.experimental import pallas as pl
from jax.experimental.pallas import tpu as pltpu
from jax.sharding import Mesh, PartitionSpec as P

LENGTH = 4096
LANES = 128
BLOCKS = LENGTH // LANES
NSEQ = 4
OCTET = 8
OCTETS = 4
GROUP = OCTET * OCTETS
SIGNALS = 2 * NSEQ + 1
ROWS = BLOCKS * OCTET
BF16 = jnp.bfloat16
F32 = jnp.float32

SPLIT = {"zh": 2, "k": 2, "y": 4, "x": 4, "zl": 2}
DP, CTX = ("zh", "k"), ("y", "x", "zl")
ORDER = ("zl", "zh", "x", "k", "y")
LEAD = tuple(SPLIT[axis] for axis in ORDER)


def make_tables():
    rows = np.arange(BLOCKS) + 0.5
    block = np.array([y * 8 + x * 2 + zl for zl in range(2) for x in range(4) for y in range(4)])
    lane = np.arange(LANES)
    eye = np.eye(OCTET)
    phase = 2.0 * math.pi * rows[:, None] * block[None, :] / (2 * BLOCKS)
    first = np.stack([np.cos(phase), -np.sin(phase)], axis=1).reshape(2 * BLOCKS, BLOCKS)
    angle = np.repeat(2.0 * math.pi * rows[:, None] * lane[None, :] / (2 * LENGTH), OCTET, axis=0)
    scale = 1.0 / (LENGTH * math.sqrt(LENGTH))
    twist = np.stack([np.cos(angle), -np.sin(angle)])
    untwist = np.stack([np.cos(angle), np.sin(angle)]) * scale
    turn = 2.0 * math.pi * (lane[:, None] * lane[None, :] % LANES) / LANES
    cosine, sine = np.cos(turn), np.sin(turn)
    second = np.block([[cosine, -sine], [sine, cosine]])
    inverse = np.block([[cosine, sine], [-sine, cosine]])
    return (
        np.kron(first, eye).astype(jnp.bfloat16),
        twist.astype(np.float32),
        second.astype(jnp.bfloat16),
        inverse.astype(jnp.bfloat16),
        untwist.astype(np.float32),
        np.kron(first.T, eye).astype(jnp.bfloat16),
    )


def dot(left, right):
    return jnp.dot(left, right, preferred_element_type=F32)


def turn_by(real, imag, turn_real, turn_imag):
    return real * turn_real - imag * turn_imag, real * turn_imag + imag * turn_real


def pair(real, imag):
    return jnp.concatenate([real, imag], axis=1).astype(BF16)


def octets(groups, first, twist, second, inverse, untwist, last):
    count = len(groups)
    gated = SIGNALS - 1
    signals = [signal for group in groups for signal in group[:gated]] + [group[gated] for group in groups]

    def index(o, s):
        return o * gated + s if s < gated else count * gated + o

    spectra = []
    for s in range(0, len(signals), 2):
        part = dot(first, jnp.concatenate(signals[s:s + 2], axis=1)).reshape(BLOCKS, 2, OCTET, 2 * LANES)
        real, imag = part[:, 0].reshape(ROWS, 2 * LANES), part[:, 1].reshape(ROWS, 2 * LANES)
        for at in range(0, 2 * LANES, LANES):
            line = pair(*turn_by(real[:, at:at + LANES], imag[:, at:at + LANES], *twist))
            spectrum = dot(line, second)
            spectra.append((spectrum[:, :LANES], spectrum[:, LANES:]))
    products = [None] * len(signals)
    for o in range(count):
        filt_real, filt_imag = spectra[index(o, gated)]
        corr_real = corr_imag = None
        for n in range(NSEQ):
            in_real, in_imag = spectra[index(o, n)]
            grad_real, grad_imag = spectra[index(o, NSEQ + n)]
            products[index(o, n)] = pair(*turn_by(in_real, in_imag, filt_real, filt_imag))
            products[index(o, NSEQ + n)] = pair(
                grad_real * filt_real + grad_imag * filt_imag, grad_imag * filt_real - grad_real * filt_imag
            )
            real = grad_real * in_real + grad_imag * in_imag
            imag = grad_imag * in_real - grad_real * in_imag
            corr_real = real if corr_real is None else corr_real + real
            corr_imag = imag if corr_imag is None else corr_imag + imag
        products[index(o, gated)] = pair(corr_real, corr_imag)
    results = []
    for s in range(0, len(signals), 2):
        columns = []
        for spectrum in products[s:s + 2]:
            line = dot(spectrum, inverse)
            real, imag = turn_by(line[:, :LANES], line[:, LANES:], *untwist)
            mixed = jnp.stack([real.reshape(BLOCKS, OCTET, LANES), imag.reshape(BLOCKS, OCTET, LANES)], axis=1)
            columns.append(mixed.reshape(2 * ROWS, LANES).astype(BF16))
        out = dot(last, jnp.concatenate(columns, axis=1))
        results += [out[:, :LANES], out[:, LANES:]]
    return [[results[index(o, s)] for s in range(SIGNALS)] for o in range(count)]


def convolve_kernel(
    x_ref, first_ref, twist_ref, second_ref, inverse_ref, untwist_ref, last_ref, y_ref, corr_ref,
):
    step = pl.program_id(0)

    def rows_of(piece):
        return piece.astype(F32).reshape(ROWS, LANES).astype(BF16)

    groups = []
    for o in range(SPLIT["k"]):
        j = step * SPLIT["k"] + o
        signals = [rows_of(x_ref[:, n // 2, :, n % 2, :, 2 * j + part]) for part in range(2) for n in range(NSEQ)]
        groups.append(signals + [rows_of(x_ref[:, step, :, o, :, 2 * OCTETS])])
    results = octets(
        groups, first_ref[...], (twist_ref[0], twist_ref[1]), second_ref[...], inverse_ref[...],
        (untwist_ref[0], untwist_ref[1]), last_ref[...],
    )
    for o, out in enumerate(results):
        out = [piece.reshape(2, 4, 4, OCTET, LANES).astype(BF16) for piece in out]
        for n in range(NSEQ):
            for part in range(2):
                y_ref[:, n // 2, :, n % 2, :, 2 * o + part] = out[part * NSEQ + n]
        for zl in range(2):
            for x in range(4):
                corr_ref[:, x, zl, o] = out[2 * NSEQ][zl, x]


def whole():
    return pl.BlockSpec(memory_space=pltpu.VMEM)


def convolve(x):
    tables = [jnp.asarray(table) for table in make_tables()]
    per = SPLIT["k"]
    return pl.pallas_call(
        convolve_kernel,
        grid=(OCTETS // per,),
        out_shape=(
            pltpu.HBM(LEAD + (2 * OCTETS, OCTET, LANES), BF16),
            jax.ShapeDtypeStruct((4, 4, 2, OCTETS, OCTET, LANES), BF16),
        ),
        in_specs=[whole()] * (1 + len(tables)),
        out_specs=(
            pl.BlockSpec(LEAD + (2 * per, OCTET, LANES), lambda j: (0, 0, 0, 0, 0, j, 0, 0)),
            pl.BlockSpec((4, 4, 2, per, OCTET, LANES), lambda j: (0, 0, 0, j, 0, 0)),
        ),
        compiler_params=pltpu.CompilerParams(vmem_limit_bytes=44 * 2**20),
        cost_estimate=pl.CostEstimate(flops=10**10, bytes_accessed=5 * 2**20, transcendentals=0),
        name="convolve",
    )(x, *tables)


def product(first, second):
    return first.astype(F32) * second.astype(F32)


def gate_kernel(
    own_ref, k_ref, v_ref, q_ref, g_ref, filt_ref, x_out, k_in, v_in, q_in, g_in, filt_in, in_sem, filt_sem,
):
    parts = SPLIT["y"]
    step = k_in.shape[0] // parts

    def arrive(y):
        at = pl.ds(y * step, step)
        refs = ((k_ref, k_in), (v_ref, v_in), (q_ref, q_in), (g_ref, g_in))
        copies = [pltpu.make_async_copy(a.at[at], b.at[at], in_sem.at[y, n]) for n, (a, b) in enumerate(refs)]
        return copies + [pltpu.make_async_copy(filt_ref.at[at, own_ref[0]], filt_in.at[at], filt_sem.at[y])]

    for y in range(parts):
        for copy in arrive(y):
            copy.start()
    for y in range(parts):
        for copy in arrive(y):
            copy.wait()
        at = pl.ds(y * step, step)
        mixed = product(k_in[at], v_in[at]).reshape(4, 2, 2, 2, GROUP, LANES)
        grad_mix = product(g_in[at], q_in[at]).reshape(4, 2, 2, 2, GROUP, LANES)
        lags = filt_in[at].reshape(4, 2, 2, 2, OCTET, LANES)
        for zl in range(2):
            for zh in range(2):
                for j in range(OCTETS):
                    rows = slice(j * OCTET, (j + 1) * OCTET)
                    x_out[zl, zh, :, :, y, 2 * j] = mixed[:, zl, zh, :, rows].astype(BF16)
                    x_out[zl, zh, :, :, y, 2 * j + 1] = grad_mix[:, zl, zh, :, rows].astype(BF16)
                x_out[zl, zh, :, :, y, 2 * OCTETS] = lags[:, zl, zh].astype(BF16)


def in_hbm(array):
    return pltpu.with_memory_space_constraint(array, pltpu.HBM)


def gate(own, k, v, q, g, filt):
    count = k.shape[0]
    parts = SPLIT["y"]
    far = pl.BlockSpec(memory_space=pltpu.HBM)
    return pl.pallas_call(
        gate_kernel,
        out_shape=jax.ShapeDtypeStruct(LEAD + (SIGNALS, OCTET, LANES), BF16),
        in_specs=[pl.BlockSpec(memory_space=pltpu.SMEM)] + [far] * 5,
        out_specs=whole(),
        scratch_shapes=[pltpu.VMEM(k.shape, BF16)] * 4
        + [
            pltpu.VMEM((count, OCTET, LANES), F32),
            pltpu.SemaphoreType.DMA((parts, 4)),
            pltpu.SemaphoreType.DMA((parts,)),
        ],
        compiler_params=pltpu.CompilerParams(vmem_limit_bytes=24 * 2**20),
        name="gate",
    )(own, *(in_hbm(array) for array in (k, v, q, g, filt)))


def ungate_kernel(
    y_ref, k_ref, v_ref, g_ref, gq_ref, gk_ref, gv_ref, k_in, v_in, g_in, gq_out, gk_out, gv_out, in_sem, out_sem,
):
    parts = SPLIT["y"]
    step = k_in.shape[0] // parts

    def arrive(i):
        at = pl.ds(i * step, step)
        refs = ((k_ref, k_in), (v_ref, v_in), (g_ref, g_in))
        return [pltpu.make_async_copy(a.at[at], b.at[at], in_sem.at[i, n]) for n, (a, b) in enumerate(refs)]

    def leave(i):
        at = pl.ds(i * step, step)
        refs = ((gq_out, gq_ref), (gk_out, gk_ref), (gv_out, gv_ref))
        return [pltpu.make_async_copy(a.at[at], b.at[at], out_sem.at[i, n]) for n, (a, b) in enumerate(refs)]

    for i in range(parts):
        for copy in arrive(i):
            copy.start()
    for i in range(parts):
        for copy in arrive(i):
            copy.wait()
        for x in range(4):
            for zl in range(2):
                for zh in range(2):
                    at = pl.ds(i * step + x * 8 + zl * 4 + zh * 2, 2)
                    conv, back = (
                        jnp.concatenate([y_ref[zl, zh, x, :, i, 2 * j + part].astype(F32) for j in range(OCTETS)], axis=1)
                        for part in range(2)
                    )
                    gq_out[at] = product(g_in[at], conv).astype(BF16)
                    gk_out[at] = product(back, v_in[at]).astype(BF16)
                    gv_out[at] = product(back, k_in[at]).astype(BF16)
        for copy in leave(i):
            copy.start()
    for i in range(parts):
        for copy in leave(i):
            copy.wait()


def ungate(y, k, v, g):
    parts = SPLIT["y"]
    far = pl.BlockSpec(memory_space=pltpu.HBM)
    return pl.pallas_call(
        ungate_kernel,
        out_shape=(pltpu.HBM(k.shape, BF16),) * 3,
        in_specs=[whole()] + [far] * 3,
        out_specs=(far,) * 3,
        scratch_shapes=[pltpu.VMEM(k.shape, BF16)] * 6 + [pltpu.SemaphoreType.DMA((parts, 3))] * 2,
        compiler_params=pltpu.CompilerParams(vmem_limit_bytes=24 * 2**20),
        cost_estimate=pl.CostEstimate(flops=0, bytes_accessed=8 * 2**20, transcendentals=0),
        name="ungate",
    )(y, *(in_hbm(array) for array in (k, v, g)))


def gather_kernel(own_ref, after_ref, r0_ref, r1_ref, r2_ref, r3_ref, corr_ref, corr_out, sem):
    del after_ref
    copies = []
    for s, piece in enumerate((r0_ref, r1_ref, r2_ref, r3_ref)):
        rows = pl.ds(pl.multiple_of((own_ref[0] ^ s) * GROUP, GROUP), GROUP)
        for p in range(BLOCKS // NSEQ):
            corr_out[s, :, p * LANES:(p + 1) * LANES] = piece[p].astype(F32)
        copies.append(pltpu.make_async_copy(corr_out.at[s], corr_ref.at[rows], sem.at[s]))
        copies[-1].start()
    for copy in copies:
        copy.wait()


def gather(own, after, pieces):
    lags = LENGTH // NSEQ
    return pl.pallas_call(
        gather_kernel,
        out_shape=pltpu.HBM((NSEQ * GROUP, lags), F32),
        in_specs=[pl.BlockSpec(memory_space=pltpu.SMEM), pl.BlockSpec(memory_space=pltpu.HBM)] + [whole()] * NSEQ,
        out_specs=pl.BlockSpec(memory_space=pltpu.HBM),
        scratch_shapes=[pltpu.VMEM((NSEQ, GROUP, lags), F32), pltpu.SemaphoreType.DMA((NSEQ,))],
        compiler_params=pltpu.CompilerParams(vmem_limit_bytes=16 * 2**20),
        name="gather",
    )(own, in_hbm(after), *pieces)


def exchange_lags(corr, own):
    quarters = corr.reshape(NSEQ, BLOCKS // NSEQ, GROUP, LANES)
    got = [lax.dynamic_index_in_dim(quarters, own, 0, keepdims=False)]
    for shift in range(1, NSEQ):
        sent = lax.dynamic_index_in_dim(quarters, own ^ shift, 0, keepdims=False)
        got.append(lax.ppermute(sent, DP, [(d, d ^ shift) for d in range(NSEQ)]))
    return got


def exchange(array):
    flat = array.reshape((-1,) + array.shape[len(LEAD):])
    return lax.all_to_all(flat, ORDER, 0, 0, tiled=True).reshape(array.shape)


def shards(q_gate, k_gate, values, grad_out, filt):
    shape = q_gate.shape
    count = shape[1] // GROUP
    q, k, v, g = (a.reshape(count, GROUP, LANES) for a in (q_gate, k_gate, values, grad_out))
    own = lax.axis_index(DP)
    slot = own.reshape(1)
    x = gate(slot, k, v, q, g, filt.reshape(count, OCTETS, OCTET, LANES))
    y, corr = convolve(exchange(x))
    pieces = exchange_lags(corr, own)
    grads = ungate(exchange(y), k, v, g)
    filter_grad = gather(slot, grads[0], pieces)
    return tuple(grad.reshape(shape) for grad in grads) + (filter_grad,)


def solution(mesh):
    split = Mesh(mesh.devices.reshape(tuple(SPLIT.values())), tuple(SPLIT))
    part = P(DP, None, CTX)
    return jax.shard_map(
        shards,
        mesh=split,
        in_specs=(part, part, part, part, P(None, CTX)),
        out_specs=(part, part, part, P(CTX, DP)),
        check_vma=False,
    )
```

```python
import math

import jax
import jax.numpy as jnp
import numpy as np
from jax import lax
from jax.experimental import pallas as pl
from jax.experimental.pallas import tpu as pltpu
from jax.sharding import Mesh, PartitionSpec as P

LENGTH = 4096
LANES = 128
BLOCKS = LENGTH // LANES
NSEQ = 4
OCTET = 8
OCTETS = 4
GROUP = OCTET * OCTETS
SIGNALS = 2 * NSEQ + 1
ROWS = BLOCKS * OCTET
BF16 = jnp.bfloat16
F32 = jnp.float32

SPLIT = {"zh": 2, "k": 2, "y": 4, "x": 4, "zl": 2}
DP, CTX = ("zh", "k"), ("y", "x", "zl")
GO = ("zl", "zh", "x", "k", "y")
BACK = ("k", "zh", "zl", "x", "y")
GO_LEAD, BACK_LEAD = (tuple(SPLIT[axis] for axis in order) for order in (GO, BACK))


def place(order, **at):
    return tuple(at.get(axis, slice(None)) for axis in order)


def taken(order):
    axes = [axis for axis in order if axis in CTX]
    weight = {"y": SPLIT["x"] * SPLIT["zl"], "x": SPLIT["zl"], "zl": 1}
    blocks = np.zeros((), int)
    for axis in axes:
        blocks = blocks[..., None] + weight[axis] * np.arange(SPLIT[axis])
    return [int(block) for block in blocks.reshape(-1)]


def make_tables():
    rows = np.arange(BLOCKS) + 0.5
    block = np.arange(BLOCKS)
    lane = np.arange(LANES)
    eye = np.eye(OCTET)
    phase = 2.0 * math.pi * rows[:, None] * block[None, :] / (2 * BLOCKS)
    first = np.stack([np.cos(phase), -np.sin(phase)], axis=1).reshape(2 * BLOCKS, BLOCKS)
    angle = np.repeat(2.0 * math.pi * rows[:, None] * lane[None, :] / (2 * LENGTH), OCTET, axis=0)
    scale = 1.0 / (LENGTH * math.sqrt(LENGTH))
    twist = np.stack([np.cos(angle), -np.sin(angle)])
    untwist = np.stack([np.cos(angle), np.sin(angle)]) * scale
    turn = 2.0 * math.pi * (lane[:, None] * lane[None, :] % LANES) / LANES
    cosine, sine = np.cos(turn), np.sin(turn)
    second = np.block([[cosine, -sine], [sine, cosine]])
    inverse = np.block([[cosine, sine], [-sine, cosine]])
    return (
        np.kron(first[:, taken(GO)], eye).astype(jnp.bfloat16),
        twist.astype(np.float32),
        second.astype(jnp.bfloat16),
        inverse.astype(jnp.bfloat16),
        untwist.astype(np.float32),
        np.kron(first[:, taken(BACK)].T, eye).astype(jnp.bfloat16),
    )


def dot(left, right):
    return jnp.dot(left, right, preferred_element_type=F32)


def turn_by(real, imag, turn_real, turn_imag):
    return real * turn_real - imag * turn_imag, real * turn_imag + imag * turn_real


def pair(real, imag):
    return jnp.concatenate([real, imag], axis=1).astype(BF16)


def octets(groups, first, twist, second, inverse, untwist, last):
    count = len(groups)
    gated = SIGNALS - 1
    signals = [signal for group in groups for signal in group[:gated]] + [group[gated] for group in groups]

    def index(o, s):
        return o * gated + s if s < gated else count * gated + o

    spectra = []
    for s in range(0, len(signals), 2):
        part = dot(first, jnp.concatenate(signals[s:s + 2], axis=1)).reshape(BLOCKS, 2, OCTET, 2 * LANES)
        real, imag = part[:, 0].reshape(ROWS, 2 * LANES), part[:, 1].reshape(ROWS, 2 * LANES)
        for at in range(0, 2 * LANES, LANES):
            line = pair(*turn_by(real[:, at:at + LANES], imag[:, at:at + LANES], *twist))
            spectrum = dot(line, second)
            spectra.append((spectrum[:, :LANES], spectrum[:, LANES:]))
    products = [None] * len(signals)
    for o in range(count):
        filt_real, filt_imag = spectra[index(o, gated)]
        corr_real = corr_imag = None
        for n in range(NSEQ):
            in_real, in_imag = spectra[index(o, n)]
            grad_real, grad_imag = spectra[index(o, NSEQ + n)]
            products[index(o, n)] = pair(*turn_by(in_real, in_imag, filt_real, filt_imag))
            products[index(o, NSEQ + n)] = pair(
                grad_real * filt_real + grad_imag * filt_imag, grad_imag * filt_real - grad_real * filt_imag
            )
            real = grad_real * in_real + grad_imag * in_imag
            imag = grad_imag * in_real - grad_real * in_imag
            corr_real = real if corr_real is None else corr_real + real
            corr_imag = imag if corr_imag is None else corr_imag + imag
        products[index(o, gated)] = pair(corr_real, corr_imag)
    results = []
    for s in range(0, len(signals), 2):
        columns = []
        for spectrum in products[s:s + 2]:
            line = dot(spectrum, inverse)
            real, imag = turn_by(line[:, :LANES], line[:, LANES:], *untwist)
            mixed = jnp.stack([real.reshape(BLOCKS, OCTET, LANES), imag.reshape(BLOCKS, OCTET, LANES)], axis=1)
            columns.append(mixed.reshape(2 * ROWS, LANES).astype(BF16))
        out = dot(last, jnp.concatenate(columns, axis=1))
        results += [out[:, :LANES], out[:, LANES:]]
    return [[results[index(o, s)] for s in range(SIGNALS)] for o in range(count)]


def convolve_kernel(
    x_ref, first_ref, twist_ref, second_ref, inverse_ref, untwist_ref, last_ref, y_ref, corr_ref,
):
    step = pl.program_id(0)
    back = tuple(SPLIT[axis] for axis in BACK if axis in CTX)

    def rows_of(piece):
        return piece.astype(F32).reshape(ROWS, LANES).astype(BF16)

    groups = []
    for o in range(SPLIT["k"]):
        j = step * SPLIT["k"] + o
        signals = [rows_of(x_ref[place(GO, zh=n // 2, k=n % 2) + (2 * j + part,)]) for part in range(2) for n in range(NSEQ)]
        groups.append(signals + [rows_of(x_ref[place(GO, zh=step, k=o) + (2 * OCTETS,)])])
    results = octets(
        groups, first_ref[...], (twist_ref[0], twist_ref[1]), second_ref[...], inverse_ref[...],
        (untwist_ref[0], untwist_ref[1]), last_ref[...],
    )
    for o, out in enumerate(results):
        out = [piece.reshape(BLOCKS, OCTET, LANES).astype(BF16) for piece in out]
        for n in range(NSEQ):
            for part in range(2):
                at = place(BACK, zh=n // 2, k=n % 2) + (2 * o + part,)
                y_ref[at] = out[part * NSEQ + n].reshape(back + (OCTET, LANES))
        for at, block in enumerate(taken(BACK)):
            corr_ref[block, o] = out[2 * NSEQ][at]


def whole():
    return pl.BlockSpec(memory_space=pltpu.VMEM)


def convolve(x):
    tables = [jnp.asarray(table) for table in make_tables()]
    per = SPLIT["k"]
    return pl.pallas_call(
        convolve_kernel,
        grid=(OCTETS // per,),
        out_shape=(
            pltpu.HBM(BACK_LEAD + (2 * OCTETS, OCTET, LANES), BF16),
            jax.ShapeDtypeStruct((BLOCKS, OCTETS, OCTET, LANES), BF16),
        ),
        in_specs=[whole()] * (1 + len(tables)),
        out_specs=(
            pl.BlockSpec(BACK_LEAD + (2 * per, OCTET, LANES), lambda j: (0, 0, 0, 0, 0, j, 0, 0)),
            pl.BlockSpec((BLOCKS, per, OCTET, LANES), lambda j: (0, j, 0, 0)),
        ),
        compiler_params=pltpu.CompilerParams(vmem_limit_bytes=44 * 2**20),
        cost_estimate=pl.CostEstimate(flops=10**10, bytes_accessed=5 * 2**20, transcendentals=0),
        name="convolve",
    )(x, *tables)


def product(first, second):
    return first.astype(F32) * second.astype(F32)


def gate_kernel(
    own_ref, k_ref, v_ref, q_ref, g_ref, filt_ref, x_out, k_in, v_in, q_in, g_in, filt_in, in_sem, filt_sem,
):
    parts = SPLIT["y"]
    step = k_in.shape[0] // parts

    def arrive(y):
        at = pl.ds(y * step, step)
        refs = ((k_ref, k_in), (v_ref, v_in), (q_ref, q_in), (g_ref, g_in))
        copies = [pltpu.make_async_copy(a.at[at], b.at[at], in_sem.at[y, n]) for n, (a, b) in enumerate(refs)]
        return copies + [pltpu.make_async_copy(filt_ref.at[at, own_ref[0]], filt_in.at[at], filt_sem.at[y])]

    for y in range(parts):
        for copy in arrive(y):
            copy.start()
    for y in range(parts):
        for copy in arrive(y):
            copy.wait()
        at = pl.ds(y * step, step)
        mixed = product(k_in[at], v_in[at]).reshape(4, 2, 2, 2, GROUP, LANES)
        grad_mix = product(g_in[at], q_in[at]).reshape(4, 2, 2, 2, GROUP, LANES)
        lags = filt_in[at].reshape(4, 2, 2, 2, OCTET, LANES)
        for zl in range(2):
            for zh in range(2):
                for k in range(2):
                    at = place(GO, zl=zl, zh=zh, k=k, y=y)
                    for j in range(OCTETS):
                        rows = slice(j * OCTET, (j + 1) * OCTET)
                        x_out[at + (2 * j,)] = mixed[:, zl, zh, k, rows].astype(BF16)
                        x_out[at + (2 * j + 1,)] = grad_mix[:, zl, zh, k, rows].astype(BF16)
                    x_out[at + (2 * OCTETS,)] = lags[:, zl, zh, k].astype(BF16)


def in_hbm(array):
    return pltpu.with_memory_space_constraint(array, pltpu.HBM)


def gate(own, k, v, q, g, filt):
    count = k.shape[0]
    parts = SPLIT["y"]
    far = pl.BlockSpec(memory_space=pltpu.HBM)
    return pl.pallas_call(
        gate_kernel,
        out_shape=jax.ShapeDtypeStruct(GO_LEAD + (SIGNALS, OCTET, LANES), BF16),
        in_specs=[pl.BlockSpec(memory_space=pltpu.SMEM)] + [far] * 5,
        out_specs=whole(),
        scratch_shapes=[pltpu.VMEM(k.shape, BF16)] * 4
        + [
            pltpu.VMEM((count, OCTET, LANES), F32),
            pltpu.SemaphoreType.DMA((parts, 4)),
            pltpu.SemaphoreType.DMA((parts,)),
        ],
        compiler_params=pltpu.CompilerParams(vmem_limit_bytes=24 * 2**20),
        name="gate",
    )(own, *(in_hbm(array) for array in (k, v, q, g, filt)))


def ungate_kernel(
    y_ref, k_ref, v_ref, g_ref, gq_ref, gk_ref, gv_ref, k_in, v_in, g_in, gq_out, gk_out, gv_out, in_sem, out_sem,
):
    parts = SPLIT["y"]
    step = k_in.shape[0] // parts

    def arrive(i):
        at = pl.ds(i * step, step)
        refs = ((k_ref, k_in), (v_ref, v_in), (g_ref, g_in))
        return [pltpu.make_async_copy(a.at[at], b.at[at], in_sem.at[i, n]) for n, (a, b) in enumerate(refs)]

    def leave(i):
        at = pl.ds(i * step, step)
        refs = ((gq_out, gq_ref), (gk_out, gk_ref), (gv_out, gv_ref))
        return [pltpu.make_async_copy(a.at[at], b.at[at], out_sem.at[i, n]) for n, (a, b) in enumerate(refs)]

    for i in range(parts):
        for copy in arrive(i):
            copy.start()
    for i in range(parts):
        for copy in arrive(i):
            copy.wait()
        for x in range(4):
            for zl in range(2):
                for zh in range(2):
                    at = pl.ds(i * step + x * 8 + zl * 4 + zh * 2, 2)
                    from_ = place(BACK, zl=zl, zh=zh, x=x, y=i)
                    conv, back = (
                        jnp.concatenate([y_ref[from_ + (2 * j + part,)].astype(F32) for j in range(OCTETS)], axis=1)
                        for part in range(2)
                    )
                    gq_out[at] = product(g_in[at], conv).astype(BF16)
                    gk_out[at] = product(back, v_in[at]).astype(BF16)
                    gv_out[at] = product(back, k_in[at]).astype(BF16)
        for copy in leave(i):
            copy.start()
    for i in range(parts):
        for copy in leave(i):
            copy.wait()


def ungate(y, k, v, g):
    parts = SPLIT["y"]
    far = pl.BlockSpec(memory_space=pltpu.HBM)
    return pl.pallas_call(
        ungate_kernel,
        out_shape=(pltpu.HBM(k.shape, BF16),) * 3,
        in_specs=[whole()] + [far] * 3,
        out_specs=(far,) * 3,
        scratch_shapes=[pltpu.VMEM(k.shape, BF16)] * 6 + [pltpu.SemaphoreType.DMA((parts, 3))] * 2,
        compiler_params=pltpu.CompilerParams(vmem_limit_bytes=24 * 2**20),
        cost_estimate=pl.CostEstimate(flops=0, bytes_accessed=8 * 2**20, transcendentals=0),
        name="ungate",
    )(y, *(in_hbm(array) for array in (k, v, g)))


def gather_kernel(own_ref, after_ref, r0_ref, r1_ref, r2_ref, r3_ref, corr_ref, corr_out, sem):
    del after_ref
    copies = []
    for s, piece in enumerate((r0_ref, r1_ref, r2_ref, r3_ref)):
        rows = pl.ds(pl.multiple_of((own_ref[0] ^ s) * GROUP, GROUP), GROUP)
        for p in range(BLOCKS // NSEQ):
            corr_out[s, :, p * LANES:(p + 1) * LANES] = piece[p].astype(F32)
        copies.append(pltpu.make_async_copy(corr_out.at[s], corr_ref.at[rows], sem.at[s]))
        copies[-1].start()
    for copy in copies:
        copy.wait()


def gather(own, after, pieces):
    lags = LENGTH // NSEQ
    return pl.pallas_call(
        gather_kernel,
        out_shape=pltpu.HBM((NSEQ * GROUP, lags), F32),
        in_specs=[pl.BlockSpec(memory_space=pltpu.SMEM), pl.BlockSpec(memory_space=pltpu.HBM)] + [whole()] * NSEQ,
        out_specs=pl.BlockSpec(memory_space=pltpu.HBM),
        scratch_shapes=[pltpu.VMEM((NSEQ, GROUP, lags), F32), pltpu.SemaphoreType.DMA((NSEQ,))],
        compiler_params=pltpu.CompilerParams(vmem_limit_bytes=16 * 2**20),
        name="gather",
    )(own, in_hbm(after), *pieces)


def exchange_lags(corr, own):
    quarters = corr.reshape(NSEQ, BLOCKS // NSEQ, GROUP, LANES)
    got = [lax.dynamic_index_in_dim(quarters, own, 0, keepdims=False)]
    for shift in range(1, NSEQ):
        sent = lax.dynamic_index_in_dim(quarters, own ^ shift, 0, keepdims=False)
        got.append(lax.ppermute(sent, DP, [(d, d ^ shift) for d in range(NSEQ)]))
    return got


def exchange(array, order):
    flat = array.reshape((-1,) + array.shape[len(order):])
    return lax.all_to_all(flat, order, 0, 0, tiled=True).reshape(array.shape)


def shards(q_gate, k_gate, values, grad_out, filt):
    shape = q_gate.shape
    count = shape[1] // GROUP
    q, k, v, g = (a.reshape(count, GROUP, LANES) for a in (q_gate, k_gate, values, grad_out))
    own = lax.axis_index(DP)
    slot = own.reshape(1)
    x = gate(slot, k, v, q, g, filt.reshape(count, OCTETS, OCTET, LANES))
    y, corr = convolve(exchange(x, GO))
    pieces = exchange_lags(corr, own)
    grads = ungate(exchange(y, BACK), k, v, g)
    filter_grad = gather(slot, grads[0], pieces)
    return tuple(grad.reshape(shape) for grad in grads) + (filter_grad,)


def solution(mesh):
    split = Mesh(mesh.devices.reshape(tuple(SPLIT.values())), tuple(SPLIT))
    part = P(DP, None, CTX)
    return jax.shard_map(
        shards,
        mesh=split,
        in_specs=(part, part, part, part, P(None, CTX)),
        out_specs=(part, part, part, P(CTX, DP)),
        check_vma=False,
    )
```

```python
import math

import jax
import jax.numpy as jnp
import numpy as np
from jax import lax
from jax.experimental import pallas as pl
from jax.experimental.pallas import tpu as pltpu
from jax.sharding import Mesh, PartitionSpec as P

LENGTH = 4096
LANES = 128
BLOCKS = LENGTH // LANES
NSEQ = 4
OCTET = 8
OCTETS = 4
GROUP = OCTET * OCTETS
SIGNALS = 2 * NSEQ + 1
ROWS = BLOCKS * OCTET
BF16 = jnp.bfloat16
F32 = jnp.float32

SPLIT = {"zh": 2, "k": 2, "y": 4, "x": 4, "zl": 2}
DP, CTX = ("zh", "k"), ("y", "x", "zl")
GO = ("zl", "zh", "x", "k", "y")
BACK = ("k", "zh", "zl", "x", "y")
GO_LEAD, BACK_LEAD = (tuple(SPLIT[axis] for axis in order) for order in (GO, BACK))


def place(order, **at):
    return tuple(at.get(axis, slice(None)) for axis in order)


def taken(order):
    axes = [axis for axis in order if axis in CTX]
    weight = {"y": SPLIT["x"] * SPLIT["zl"], "x": SPLIT["zl"], "zl": 1}
    blocks = np.zeros((), int)
    for axis in axes:
        blocks = blocks[..., None] + weight[axis] * np.arange(SPLIT[axis])
    return [int(block) for block in blocks.reshape(-1)]


def make_tables():
    rows = np.arange(BLOCKS) + 0.5
    block = np.arange(BLOCKS)
    lane = np.arange(LANES)
    eye = np.eye(OCTET)
    phase = 2.0 * math.pi * rows[:, None] * block[None, :] / (2 * BLOCKS)
    first = np.stack([np.cos(phase), -np.sin(phase)], axis=1).reshape(2 * BLOCKS, BLOCKS)
    angle = np.repeat(2.0 * math.pi * rows[:, None] * lane[None, :] / (2 * LENGTH), OCTET, axis=0)
    scale = 1.0 / (LENGTH * math.sqrt(LENGTH))
    twist = np.stack([np.cos(angle), -np.sin(angle)])
    untwist = np.stack([np.cos(angle), np.sin(angle)]) * scale
    turn = 2.0 * math.pi * (lane[:, None] * lane[None, :] % LANES) / LANES
    cosine, sine = np.cos(turn), np.sin(turn)
    second = np.block([[cosine, -sine], [sine, cosine]])
    inverse = np.block([[cosine, sine], [-sine, cosine]])
    return (
        np.kron(first[:, taken(GO)], eye).astype(jnp.bfloat16),
        twist.astype(np.float32),
        second.astype(jnp.bfloat16),
        inverse.astype(jnp.bfloat16),
        untwist.astype(np.float32),
        np.kron(first[:, taken(BACK)].T, eye).astype(jnp.bfloat16),
    )


def dot(left, right):
    return jnp.dot(left, right, preferred_element_type=F32)


def turn_by(real, imag, turn_real, turn_imag):
    return real * turn_real - imag * turn_imag, real * turn_imag + imag * turn_real


def pair(real, imag):
    return jnp.concatenate([real, imag], axis=1).astype(BF16)


def octets(groups, first, twist, second, inverse, untwist, last):
    count = len(groups)
    gated = SIGNALS - 1
    signals = [signal for group in groups for signal in group[:gated]] + [group[gated] for group in groups]

    def index(o, s):
        return o * gated + s if s < gated else count * gated + o

    spectra = []
    for s in range(0, len(signals), 2):
        part = dot(first, jnp.concatenate(signals[s:s + 2], axis=1)).reshape(BLOCKS, 2, OCTET, 2 * LANES)
        real, imag = part[:, 0].reshape(ROWS, 2 * LANES), part[:, 1].reshape(ROWS, 2 * LANES)
        for at in range(0, 2 * LANES, LANES):
            line = pair(*turn_by(real[:, at:at + LANES], imag[:, at:at + LANES], *twist))
            spectrum = dot(line, second)
            spectra.append((spectrum[:, :LANES], spectrum[:, LANES:]))
    products = [None] * len(signals)
    for o in range(count):
        filt_real, filt_imag = spectra[index(o, gated)]
        corr_real = corr_imag = None
        for n in range(NSEQ):
            in_real, in_imag = spectra[index(o, n)]
            grad_real, grad_imag = spectra[index(o, NSEQ + n)]
            products[index(o, n)] = pair(*turn_by(in_real, in_imag, filt_real, filt_imag))
            products[index(o, NSEQ + n)] = pair(
                grad_real * filt_real + grad_imag * filt_imag, grad_imag * filt_real - grad_real * filt_imag
            )
            real = grad_real * in_real + grad_imag * in_imag
            imag = grad_imag * in_real - grad_real * in_imag
            corr_real = real if corr_real is None else corr_real + real
            corr_imag = imag if corr_imag is None else corr_imag + imag
        products[index(o, gated)] = pair(corr_real, corr_imag)
    results = []
    for s in range(0, len(signals), 2):
        columns = []
        for spectrum in products[s:s + 2]:
            line = dot(spectrum, inverse)
            real, imag = turn_by(line[:, :LANES], line[:, LANES:], *untwist)
            mixed = jnp.stack([real.reshape(BLOCKS, OCTET, LANES), imag.reshape(BLOCKS, OCTET, LANES)], axis=1)
            columns.append(mixed.reshape(2 * ROWS, LANES).astype(BF16))
        out = dot(last, jnp.concatenate(columns, axis=1))
        results += [out[:, :LANES], out[:, LANES:]]
    return [[results[index(o, s)] for s in range(SIGNALS)] for o in range(count)]


def convolve_kernel(
    x_ref, first_ref, twist_ref, second_ref, inverse_ref, untwist_ref, last_ref, y_ref, corr_ref,
):
    step = pl.program_id(0)
    back = tuple(SPLIT[axis] for axis in BACK if axis in CTX)

    def rows_of(piece):
        return piece.astype(F32).reshape(ROWS, LANES).astype(BF16)

    groups = []
    for o in range(SPLIT["k"]):
        j = step * SPLIT["k"] + o
        signals = [rows_of(x_ref[place(GO, zh=n // 2, k=n % 2) + (2 * j + part,)]) for part in range(2) for n in range(NSEQ)]
        groups.append(signals + [rows_of(x_ref[place(GO, zh=step, k=o) + (2 * OCTETS,)])])
    results = octets(
        groups, first_ref[...], (twist_ref[0], twist_ref[1]), second_ref[...], inverse_ref[...],
        (untwist_ref[0], untwist_ref[1]), last_ref[...],
    )
    for o, out in enumerate(results):
        out = [piece.reshape(BLOCKS, OCTET, LANES).astype(BF16) for piece in out]
        for n in range(NSEQ):
            for part in range(2):
                at = place(BACK, zh=n // 2, k=n % 2) + (2 * o + part,)
                y_ref[at] = out[part * NSEQ + n].reshape(back + (OCTET, LANES))
        for at, block in enumerate(taken(BACK)):
            corr_ref[block, o] = out[2 * NSEQ][at]


def whole():
    return pl.BlockSpec(memory_space=pltpu.VMEM)


def convolve(x):
    tables = [jnp.asarray(table) for table in make_tables()]
    per = SPLIT["k"]
    return pl.pallas_call(
        convolve_kernel,
        grid=(OCTETS // per,),
        out_shape=(
            pltpu.HBM(BACK_LEAD + (2 * OCTETS, OCTET, LANES), BF16),
            jax.ShapeDtypeStruct((BLOCKS, OCTETS, OCTET, LANES), BF16),
        ),
        in_specs=[whole()] * (1 + len(tables)),
        out_specs=(
            pl.BlockSpec(BACK_LEAD + (2 * per, OCTET, LANES), lambda j: (0, 0, 0, 0, 0, j, 0, 0)),
            pl.BlockSpec((BLOCKS, per, OCTET, LANES), lambda j: (0, j, 0, 0)),
        ),
        compiler_params=pltpu.CompilerParams(vmem_limit_bytes=44 * 2**20),
        cost_estimate=pl.CostEstimate(flops=10**10, bytes_accessed=5 * 2**20, transcendentals=0),
        name="convolve",
    )(x, *tables)


def product(first, second):
    return first.astype(F32) * second.astype(F32)


def gate_kernel(
    own_ref, k_ref, v_ref, q_ref, g_ref, filt_ref, x_out, k_in, v_in, q_in, g_in, filt_in, in_sem, filt_sem,
):
    parts = SPLIT["y"]
    step = k_in.shape[0] // parts

    def arrive(y):
        at = pl.ds(y * step, step)
        refs = ((k_ref, k_in), (v_ref, v_in), (q_ref, q_in), (g_ref, g_in))
        copies = [pltpu.make_async_copy(a.at[at], b.at[at], in_sem.at[y, n]) for n, (a, b) in enumerate(refs)]
        return copies + [pltpu.make_async_copy(filt_ref.at[at, own_ref[0]], filt_in.at[at], filt_sem.at[y])]

    for y in range(parts):
        for copy in arrive(y):
            copy.start()
    for y in range(parts):
        for copy in arrive(y):
            copy.wait()
        at = pl.ds(y * step, step)
        mixed = product(k_in[at], v_in[at]).reshape(4, 2, 2, 2, GROUP, LANES)
        grad_mix = product(g_in[at], q_in[at]).reshape(4, 2, 2, 2, GROUP, LANES)
        lags = filt_in[at].reshape(4, 2, 2, 2, OCTET, LANES)
        for zl in range(2):
            for zh in range(2):
                for k in range(2):
                    at = place(GO, zl=zl, zh=zh, k=k, y=y)
                    for j in range(OCTETS):
                        rows = slice(j * OCTET, (j + 1) * OCTET)
                        x_out[at + (2 * j,)] = mixed[:, zl, zh, k, rows].astype(BF16)
                        x_out[at + (2 * j + 1,)] = grad_mix[:, zl, zh, k, rows].astype(BF16)
                    x_out[at + (2 * OCTETS,)] = lags[:, zl, zh, k].astype(BF16)


def in_hbm(array):
    return pltpu.with_memory_space_constraint(array, pltpu.HBM)


def gate(own, k, v, q, g, filt):
    count = k.shape[0]
    parts = SPLIT["y"]
    far = pl.BlockSpec(memory_space=pltpu.HBM)
    return pl.pallas_call(
        gate_kernel,
        out_shape=jax.ShapeDtypeStruct(GO_LEAD + (SIGNALS, OCTET, LANES), BF16),
        in_specs=[pl.BlockSpec(memory_space=pltpu.SMEM)] + [far] * 5,
        out_specs=whole(),
        scratch_shapes=[pltpu.VMEM(k.shape, BF16)] * 4
        + [
            pltpu.VMEM((count, OCTET, LANES), F32),
            pltpu.SemaphoreType.DMA((parts, 4)),
            pltpu.SemaphoreType.DMA((parts,)),
        ],
        compiler_params=pltpu.CompilerParams(vmem_limit_bytes=24 * 2**20),
        name="gate",
    )(own, *(in_hbm(array) for array in (k, v, q, g, filt)))


def ungate_kernel(
    y_ref, k_ref, v_ref, g_ref, gq_ref, gk_ref, gv_ref, k_in, v_in, g_in, gq_out, gk_out, gv_out, in_sem, out_sem,
):
    parts = SPLIT["y"]
    step = k_in.shape[0] // parts

    def arrive(i):
        at = pl.ds(i * step, step)
        refs = ((k_ref, k_in), (v_ref, v_in), (g_ref, g_in))
        return [pltpu.make_async_copy(a.at[at], b.at[at], in_sem.at[i, n]) for n, (a, b) in enumerate(refs)]

    def leave(i):
        at = pl.ds(i * step, step)
        refs = ((gq_out, gq_ref), (gk_out, gk_ref), (gv_out, gv_ref))
        return [pltpu.make_async_copy(a.at[at], b.at[at], out_sem.at[i, n]) for n, (a, b) in enumerate(refs)]

    for i in range(parts):
        for copy in arrive(i):
            copy.start()
    for i in range(parts):
        for copy in arrive(i):
            copy.wait()
        for x in range(4):
            for zl in range(2):
                for zh in range(2):
                    at = pl.ds(i * step + x * 8 + zl * 4 + zh * 2, 2)
                    from_ = place(BACK, zl=zl, zh=zh, x=x, y=i)
                    conv, back = (
                        jnp.concatenate([y_ref[from_ + (2 * j + part,)].astype(F32) for j in range(OCTETS)], axis=1)
                        for part in range(2)
                    )
                    gq_out[at] = product(g_in[at], conv).astype(BF16)
                    gk_out[at] = product(back, v_in[at]).astype(BF16)
                    gv_out[at] = product(back, k_in[at]).astype(BF16)
        for copy in leave(i):
            copy.start()
    for i in range(parts):
        for copy in leave(i):
            copy.wait()


def ungate(y, k, v, g):
    parts = SPLIT["y"]
    far = pl.BlockSpec(memory_space=pltpu.HBM)
    return pl.pallas_call(
        ungate_kernel,
        out_shape=(pltpu.HBM(k.shape, BF16),) * 3,
        in_specs=[whole()] + [far] * 3,
        out_specs=(far,) * 3,
        scratch_shapes=[pltpu.VMEM(k.shape, BF16)] * 6 + [pltpu.SemaphoreType.DMA((parts, 3))] * 2,
        compiler_params=pltpu.CompilerParams(vmem_limit_bytes=24 * 2**20),
        cost_estimate=pl.CostEstimate(flops=0, bytes_accessed=8 * 2**20, transcendentals=0),
        name="ungate",
    )(y, *(in_hbm(array) for array in (k, v, g)))


def gather_kernel(own_ref, after_ref, r0_ref, r1_ref, r2_ref, r3_ref, corr_ref):
    del after_ref
    for s, piece in enumerate((r0_ref, r1_ref, r2_ref, r3_ref)):
        rows = pl.ds(pl.multiple_of((own_ref[0] ^ s) * GROUP, GROUP), GROUP)
        for p in range(BLOCKS // NSEQ):
            corr_ref[rows, p * LANES:(p + 1) * LANES] = piece[p].astype(F32)


def gather(own, after, pieces):
    lags = LENGTH // NSEQ
    return pl.pallas_call(
        gather_kernel,
        out_shape=pltpu.HBM((NSEQ * GROUP, lags), F32),
        in_specs=[pl.BlockSpec(memory_space=pltpu.SMEM), pl.BlockSpec(memory_space=pltpu.HBM)] + [whole()] * NSEQ,
        out_specs=pl.BlockSpec((NSEQ * GROUP, lags), lambda: (0, 0)),
        compiler_params=pltpu.CompilerParams(vmem_limit_bytes=16 * 2**20),
        name="gather",
    )(own, in_hbm(after), *pieces)


def exchange_lags(corr, own):
    quarters = corr.reshape(NSEQ, BLOCKS // NSEQ, GROUP, LANES)
    got = [lax.dynamic_index_in_dim(quarters, own, 0, keepdims=False)]
    for shift in range(1, NSEQ):
        sent = lax.dynamic_index_in_dim(quarters, own ^ shift, 0, keepdims=False)
        got.append(lax.ppermute(sent, DP, [(d, d ^ shift) for d in range(NSEQ)]))
    return got


def exchange(array, order):
    flat = array.reshape((-1,) + array.shape[len(order):])
    return lax.all_to_all(flat, order, 0, 0, tiled=True).reshape(array.shape)


def shards(q_gate, k_gate, values, grad_out, filt):
    shape = q_gate.shape
    count = shape[1] // GROUP
    q, k, v, g = (a.reshape(count, GROUP, LANES) for a in (q_gate, k_gate, values, grad_out))
    own = lax.axis_index(DP)
    slot = own.reshape(1)
    x = gate(slot, k, v, q, g, filt.reshape(count, OCTETS, OCTET, LANES))
    y, corr = convolve(exchange(x, GO))
    pieces = exchange_lags(corr, own)
    grads = ungate(exchange(y, BACK), k, v, g)
    filter_grad = gather(slot, grads[0], pieces)
    return tuple(grad.reshape(shape) for grad in grads) + (filter_grad,)


def solution(mesh):
    split = Mesh(mesh.devices.reshape(tuple(SPLIT.values())), tuple(SPLIT))
    part = P(DP, None, CTX)
    return jax.shard_map(
        shards,
        mesh=split,
        in_specs=(part, part, part, part, P(None, CTX)),
        out_specs=(part, part, part, P(CTX, DP)),
        check_vma=False,
    )
```
